512 devices in a mesh: seq: 32 (over x, y), head: 16 (over z, core).
Axes of the slice: x: 4, y: 8, z: 8, core: 2. Of those that a mesh axis runs over, the one named last changes fastest.
Arguments:
- tokens: bfloat16 [8192, 2048], P('seq'), may hold values from -18 to 18
- qkv_weight: bfloat16 [3, 2048, 2048], P(None, None, 'head'), may hold values from -1 to 1
- beta_logit: float32 [16, 8192], P('head', 'seq'), may hold values from -5.8 to -3.5
- log_decay: float32 [16, 8192], P('head', 'seq'), may hold values from -1 to 0
- out_grad: bfloat16 [8192, 2048], P('seq', 'head'), may hold values from -24 to 24
Outputs:
- input_grad: bfloat16 [8192, 2048], P('seq', 'head')
The draws below stay inside these ranges and needn't reach their ends.
All inputs are finite; a program needn't handle non-finite values.
Results may differ from the reference program's by a relative error of at most 0.008.
Values may be sent and summed in bfloat16 or wider, within the bound.
A program may use at most 64 MiB of HBM per device.

```python
import math
import jax
import jax.numpy as jnp
from jax import lax

D = 2048
HEADS = 16
DK = 128
TOK_DEV = 256
TOKENS = 8192


def draw_tokens(key, part):
    streams = jax.random.split(key, 2)
    scales = jnp.exp(jax.random.uniform(streams[0], (TOKENS, 1), jnp.float32, math.log(0.3), math.log(3.0)))
    entries = jnp.clip(jax.random.normal(streams[1], (TOKENS, D), jnp.float32), -6.0, 6.0)
    return (scales * entries).astype(jnp.bfloat16)


def draw_qkv_weight(key, part):
    streams = jax.random.split(key, 2)
    column_scales = jnp.exp(jax.random.uniform(streams[0], (3, 1, HEADS * DK), jnp.float32, math.log(0.32), math.log(3.2)))
    base = jnp.clip(jax.random.normal(streams[1], (3, D, HEADS * DK), jnp.float32), -2.5, 2.5)
    return (base * column_scales / math.sqrt(D)).astype(jnp.bfloat16)


def draw_log_decay(key, part):
    streams = jax.random.split(key, 7)
    share = 0.5
    slow_heads = jax.random.uniform(streams[0], (HEADS, 1), jnp.float32) < share
    fast_rate = jnp.exp(jax.random.uniform(streams[1], (HEADS, 1), jnp.float32, math.log(1.0 / 50.0), math.log(1.0 / 30.0)))
    slow_rate = jnp.exp(jax.random.uniform(streams[2], (HEADS, 1), jnp.float32, math.log(0.05), math.log(0.3))) / TOKENS
    forget_factors = jnp.where(slow_heads, slow_rate, fast_rate)
    piece_scaling_factor = jnp.exp(jax.random.uniform(streams[3], (HEADS, TOKENS // TOK_DEV), jnp.float32, math.log(0.5), math.log(2.0)))
    piece_scaling_factor = jnp.repeat(piece_scaling_factor, TOK_DEV, axis=1)
    element_scaling_factor = jax.random.uniform(streams[4], (HEADS, TOKENS), jnp.float32, 0.5, 1.5)
    element_slots = jax.random.randint(streams[5], (2, 1), 0, TOKENS)
    element_offsets = jnp.arange(TOKENS)[None, :]
    piece_groupings = jnp.sum((element_offsets == element_slots).astype(jnp.float32), axis=0)[None, :]
    objective_scores = jax.random.uniform(streams[6], (HEADS, TOKENS), jnp.float32, 0.22, 0.4)
    return -forget_factors * piece_scaling_factor * element_scaling_factor - piece_groupings * objective_scores


def block_scale(rng, dims, shards, smallest, largest):
    def one(position, blocks):
        heights = jax.random.uniform(jax.random.fold_in(jax.random.fold_in(rng, 6), position), (blocks,), jnp.float32, smallest / len(shards), largest / len(shards))
        return jnp.repeat(jnp.exp(heights), dims[position] // blocks).reshape((-1,) + (1,) * (len(dims) - position - 1))

    level = one(*shards[0])
    for cut in shards[1:]:
        level = level * one(*cut)
    return level


def scatter_about(rng, dims, deviation, limit, cuts=(), kind=jnp.bfloat16):
    values = deviation * jax.random.normal(rng, dims, jnp.float32)
    if cuts:
        values = values * block_scale(rng, dims, cuts, -0.22, 0.18)
    return jnp.clip(values, -limit, limit).astype(kind)


def setup_inputs(seed: int = 0) -> dict:
    streams_of = jax.random.split(jax.random.key(seed), 6)
    return {
        "tokens": draw_tokens(jax.random.fold_in(streams_of[5], 71), 0),
        "qkv_weight": draw_qkv_weight(jax.random.fold_in(streams_of[5], 71), 0),
        "beta_logit": jnp.clip(-5.8 + 2.3000002 * jax.random.uniform(streams_of[2], (HEADS, TOKENS), jnp.float32) ** block_scale(streams_of[2], (HEADS, TOKENS), ((0, 16), (1, 32)), -0.2, 0.2), -5.8, -3.5),
        "log_decay": draw_log_decay(jax.random.fold_in(streams_of[5], 71), 0),
        "out_grad": scatter_about(streams_of[4], (TOKENS, HEADS * DK), 4.0, 24.0, ((0, 32), (1, 16))),
    }


HIGH = lax.Precision.HIGHEST
block_tokens = 64

def unit_rows(tensor):
    return tensor * lax.rsqrt(lax.optimization_barrier(jnp.sum(tensor * tensor, axis=-1, keepdims=True)) + 1e-06)

def head_grad(queries, key_rows, values, log_decay, strengths, cotangent):
    length, head_width = queries.shape
    block_size = min(block_tokens, length)
    blocks = length // block_size

    def advance(memory, inputs):
        query_row, key_row, value_row, decay_row, strength_row = inputs
        kept = jnp.exp(decay_row) * memory
        recall = jnp.dot(key_row, kept, precision=HIGH)
        memory = kept + strength_row * jnp.outer(key_row, value_row - recall)
        return (memory, jnp.dot(query_row, memory, precision=HIGH))

    def run_block(memory, inputs):
        return lax.scan(advance, memory, inputs)
    checked = jax.checkpoint(run_block)

    def forward(query_in, key_in, value_in):
        unit_query = unit_rows(query_in)
        unit_key = unit_rows(key_in)
        pieces = (unit_query, unit_key, value_in, log_decay, strengths)
        blocked = tuple((tensor.reshape((blocks, block_size) + tensor.shape[1:]) for tensor in pieces))
        zeroed = jnp.zeros((head_width, head_width), jnp.float32)
        _, results = lax.scan(checked, zeroed, blocked)
        return results.reshape(length, head_width)
    _, pullback = jax.vjp(forward, queries, key_rows, values)
    return pullback(cotangent)

def reference(tokens, qkv_weight, beta_logit, log_decay, out_grad):
    total_rows = tokens.shape[0]
    heads = beta_logit.shape[0]
    head_width = qkv_weight.shape[-1] // heads

    def per_head(tensor):
        return tensor.reshape(total_rows, heads, head_width).transpose(1, 0, 2)
    projected = [per_head(jnp.dot(tokens, qkv_weight[member], preferred_element_type=jnp.float32)) for member in range(3)]
    strengths = jax.nn.sigmoid(beta_logit)
    cotangent = per_head(out_grad.astype(jnp.float32))

    def one_head(pieces):
        return head_grad(pieces[0], pieces[1], pieces[2], pieces[3], pieces[4], pieces[5])
    grads = lax.map(one_head, (projected[0], projected[1], projected[2], log_decay, strengths, cotangent))
    result = jnp.zeros((total_rows, tokens.shape[1]), jnp.float32)
    for member in range(3):
        flat = grads[member].transpose(1, 0, 2).reshape(total_rows, heads * head_width)
        weight_full = qkv_weight[member].astype(jnp.float32)
        result = result + jnp.dot(flat, weight_full.T, precision=HIGH)
    return result.astype(jnp.bfloat16)
```

```python
import functools

import jax
import jax.numpy as jnp
from jax import lax
from jax.experimental import pallas as pl
from jax.experimental.pallas import tpu as pltpu
from jax.sharding import PartitionSpec as P

F32 = jnp.float32
BF16 = jnp.bfloat16
MESH = pl.DeviceIdType.MESH
X, Y, Z = 4, 8, 8
C, DK = 256, 128
B_AT, R_AT, A_AT, Z_AT, ROWS = 0, 128, 256, 272, 400
PIECES = ((R_AT, 144), (B_AT, 128), (Z_AT, 128))


def dot(a, b, ca=1, cb=0):
    return lax.dot_general(
        a.astype(BF16), b.astype(BF16), (((ca,), (cb,)), ((), ())), preferred_element_type=F32
    )


def split(a):
    upper = a.astype(BF16)
    return upper, (a - upper.astype(F32)).astype(BF16)


def thirds(a):
    upper, rest = split(a)
    middle = rest
    lower = (a - upper.astype(F32) - middle.astype(F32)).astype(BF16)
    return upper, middle, lower


def unit_inverse_less_identity(low, rows, cols):
    def same(shift):
        return (rows >> shift) == (cols >> shift)

    power = jnp.where(same(5), low, 0.0)
    off = -power
    for _ in range(4):
        power = dot(power, power)
        off = off + power + dot(off, power)
    for shift in (5, 6, 7):
        inside = jnp.where(same(shift + 1) & ~same(shift), low, 0.0)
        left = inside + dot(off, inside)
        off = off - left - dot(left, off)
    return off


def kernel(
    tok, wgt, bl, ld, og, out,
    ag, xg, pre, core_out, core_in, own, up_out, dn_out, up_in, dn_in, fin,
    up_s, up_r, dn_s, dn_r, x_s, x_r, c_s, c_r, zu_s, zu_r, zd_s, zd_r,
):
    seq, head = lax.axis_index("seq"), lax.axis_index("head")
    x, y = seq // Y, seq % Y
    z, core = head // 2, head % 2

    def at(dx=0, dy=0, dz=0, dc=0):
        return (
            ((x + dx) % X) * Y + (y + dy + Y) % Y,
            ((z + dz + Z) % Z) * 2 + (core + dc) % 2,
        )

    peers = [at(dy=1), at(dy=-1), at(dx=1), at(dx=2), at(dx=3), at(dc=1), at(dz=1), at(dz=-1)]
    barrier = pltpu.get_barrier_semaphore()
    for peer in peers:
        pl.semaphore_signal(barrier, inc=1, device_id=peer, device_id_type=MESH)

    proj = [
        lax.dot_general(tok[...], wgt[p], (((1,), (0,)), ((), ())), preferred_element_type=F32)
        for p in range(3)
    ]
    q_inv = lax.rsqrt(jnp.sum(proj[0] * proj[0], axis=1, keepdims=True) + 1e-6)
    k_inv = lax.rsqrt(jnp.sum(proj[1] * proj[1], axis=1, keepdims=True) + 1e-6)
    qn, kn, v = proj[0] * q_inv, proj[1] * k_inv, proj[2]
    g = og[...]
    rows = lax.broadcasted_iota(jnp.int32, (C, C), 0)
    cols = lax.broadcasted_iota(jnp.int32, (C, C), 1)
    beta_row = 1.0 / (1.0 + jnp.exp(-bl[...]))
    beta = jnp.sum(jnp.where(rows == cols, beta_row, 0.0), axis=1, keepdims=True)
    cum = jnp.sum(jnp.where(cols <= rows, ld[...], 0.0), axis=1, keepdims=True)
    cum_row = jnp.sum(jnp.where(rows == cols, cum, 0.0), axis=0, keepdims=True)
    total = cum[C - 1 : C, :]
    decay = jnp.exp(-jnp.abs(cum - cum_row))
    opening = jnp.exp(cum)
    fading = jnp.exp(total - cum)
    causal, anti = rows >= cols, rows <= cols

    kb = kn.astype(BF16)
    qb = qn.astype(BF16)
    low = beta * jnp.where(rows > cols, decay * dot(kb, kb, 1, 1), 0.0)
    off = unit_inverse_less_identity(low, rows, cols).astype(BF16)
    bk = opening * kn
    fk = fading * kn
    x0 = beta * bk
    xs = x0 + dot(off, x0)
    xf = beta * (fk + dot(off, fk, 0, 0))
    v0 = beta * v
    w0 = v0 + dot(off, v0)
    pg = dot(jnp.where(anti, decay * dot(kb, qb, 1, 1), 0.0), g)
    y0 = beta * (pg + dot(off, pg, 0, 0))
    fk_hi, fk_lo = split(fk)
    w_hi, w_lo = split(w0)
    b_seg = dot(fk_hi, w_hi, 0, 0) + (dot(fk_lo, w_hi, 0, 0) + dot(fk_hi, w_lo, 0, 0))
    z_seg = dot(opening * qn, g, 0, 0) - dot(xs, pg, 0, 0)
    r_seg = -dot(xf, bk, 0, 0)
    a_seg = jnp.broadcast_to(jnp.exp(total), (1, DK))

    def put(ref, a, r, b, zz):
        ref[pl.ds(B_AT, DK), :] = b.astype(BF16)
        ref[pl.ds(R_AT, DK), :] = r.astype(BF16)
        ref[pl.ds(Z_AT, DK), :] = zz.astype(BF16)
        place = lax.broadcasted_iota(jnp.int32, (16, DK), 0)
        first, second, third = [t.astype(F32) for t in thirds(a)]
        tile = jnp.where(place == 0, first, jnp.where(place == 1, second, jnp.where(place == 2, third, 0.0)))
        ref[pl.ds(A_AT, 16), :] = tile.astype(BF16)

    def scale_of(ref):
        return jnp.sum(ref[pl.ds(A_AT, 16), :].astype(F32), axis=0, keepdims=True)

    put(ag.at[y], a_seg, r_seg, b_seg, z_seg)
    pl.semaphore_wait(barrier, len(peers))

    def y_copy(step, piece, up):
        slot = (y - step + Y) % Y if up else (y + step) % Y
        start, size = PIECES[piece]
        part = ag.at[slot, pl.ds(start, size)]
        ss, rs = (up_s, up_r) if up else (dn_s, dn_r)
        return pltpu.make_async_remote_copy(
            src_ref=part, dst_ref=part, send_sem=ss.at[step, piece], recv_sem=rs.at[step, piece],
            device_id=at(dy=1) if up else at(dy=-1), device_id_type=MESH,
        )

    def y_arrived(step, piece, up):
        slot = (y - step - 1 + Y) % Y if up else (y + step + 1) % Y
        start, size = PIECES[piece]
        part = ag.at[slot, pl.ds(start, size)]
        ss, rs = (up_s, up_r) if up else (dn_s, dn_r)
        pltpu.make_async_remote_copy(
            src_ref=part, dst_ref=part, send_sem=ss.at[step, piece], recv_sem=rs.at[step, piece],
            device_id=at(dy=1) if up else at(dy=-1), device_id_type=MESH,
        ).wait_recv()

    for step in range(5):
        for piece in range(3):
            for up, steps in ((True, 4), (False, 3)):
                if 1 <= step <= steps:
                    y_arrived(step - 1, piece, up)
                if step < steps:
                    y_copy(step, piece, up).start()

    fwd_a = jnp.ones((1, DK), F32)
    fwd = jnp.zeros((DK, 2 * DK), F32)
    bwd_a = jnp.ones((1, DK), F32)
    bwd = jnp.zeros((DK, 2 * DK), F32)

    def twice(row):
        return jnp.concatenate([row, row], axis=1)

    eye = (
        lax.broadcasted_iota(jnp.int32, (DK, DK), 0) == lax.broadcasted_iota(jnp.int32, (DK, DK), 1)
    ).astype(F32)
    for turn in range(Y):
        j, i = turn, Y - 1 - turn

        @pl.when(y == j)
        def _(fwd=fwd, fwd_a=fwd_a):
            pre[0] = fwd
            pre[2, 0:1, 0:DK] = fwd_a

        @pl.when(y == i)
        def _(bwd=bwd, bwd_a=bwd_a):
            pre[1] = bwd
            pre[2, 8:9, 0:DK] = bwd_a

        a_j, r_j = scale_of(ag.at[j]), ag[j, pl.ds(R_AT, DK), :]
        b_j = ag[j, pl.ds(B_AT, DK), :].astype(F32)
        fwd = (
            twice(a_j) * fwd
            + dot(r_j, fwd)
            + jnp.concatenate([fwd_a * r_j.astype(F32), b_j], axis=1)
        )
        fwd_a = fwd_a * a_j
        a_i, r_i = scale_of(ag.at[i]), ag[i, pl.ds(R_AT, DK), :]
        z_i = ag[i, pl.ds(Z_AT, DK), :].astype(F32)
        r_it = dot(r_i, eye, 0, 0)
        bwd = (
            twice(a_i) * bwd
            + dot(r_it, bwd)
            + jnp.concatenate([bwd_a * r_it, z_i], axis=1)
        )
        bwd_a = bwd_a * a_i

    put(xg.at[x], fwd_a, fwd[:, :DK], fwd[:, DK:], bwd[:, DK:])
    x_copies = []
    for m in range(1, X):
        start = pl.multiple_of(jnp.where(x + m < X, B_AT, R_AT), 128)
        part = xg.at[x, pl.ds(start, 272)]
        x_copies.append(
            pltpu.make_async_remote_copy(
                src_ref=part, dst_ref=part, send_sem=x_s.at[m], recv_sem=x_r.at[m],
                device_id=at(dx=m), device_id_type=MESH,
            )
        )
        x_copies[-1].start()
    for m in range(1, X):
        source = (x - m + X) % X
        start = pl.multiple_of(jnp.where(source < x, B_AT, R_AT), 128)
        part = xg.at[source, pl.ds(start, 272)]
        pltpu.make_async_remote_copy(
            src_ref=part, dst_ref=part, send_sem=x_s.at[m], recv_sem=x_r.at[m],
            device_id=at(dx=m), device_id_type=MESH,
        ).wait_recv()
    state, seed = fin.at[0], fin.at[1]
    state[...] = jnp.zeros((DK, DK), F32)
    seed[...] = jnp.zeros((DK, DK), F32)
    for j in range(X - 1):
        i = X - 1 - j

        @pl.when(j < x)
        def _():
            old = state[...]
            state[...] = (
                scale_of(xg.at[j]) * old
                + dot(xg[j, pl.ds(R_AT, DK), :], old)
                + xg[j, pl.ds(B_AT, DK), :].astype(F32)
            )

        @pl.when(i > x)
        def _():
            old = seed[...]
            seed[...] = (
                scale_of(xg.at[i]) * old
                + dot(xg[i, pl.ds(R_AT, DK), :], old, 0, 0)
                + xg[i, pl.ds(Z_AT, DK), :].astype(F32)
            )

    old = state[...]
    s_in = pre[2, 0:1, 0:DK] * old + dot(pre[0, :, 0:DK], old) + pre[0, :, DK : 2 * DK]
    old = seed[...]
    g_out = pre[2, 8:9, 0:DK] * old + dot(pre[1, :, 0:DK], old) + pre[1, :, DK : 2 * DK]

    w = w0 - dot(xs, s_in)
    yy = y0 + dot(xf, g_out)
    wb, yb = w.astype(BF16), yy.astype(BF16)
    s_hi, s_lo = split(s_in)
    e = jnp.where(causal, decay * dot(g, wb, 1, 1), 0.0)
    et = jnp.where(anti, decay * dot(wb, g, 1, 1), 0.0)
    h = jnp.where(rows > cols, dot(yb, wb, 1, 1), dot(wb, yb, 1, 1)) * decay
    h = jnp.where(rows == cols, 0.0, h)
    dq = opening * (dot(g, s_hi, 1, 1) + dot(g, s_lo, 1, 1)) + dot(e, kb)
    dk = fading * dot(wb, g_out, 1, 1) + dot(et, qb) - dot(h, kb) - opening * dot(yb, s_hi, 1, 1)
    dq = q_inv * (dq - qn * jnp.sum(qn * dq, axis=1, keepdims=True))
    dk = k_inv * (dk - kn * jnp.sum(kn * dk, axis=1, keepdims=True))
    grads = [split(t) for t in (dq, dk, yy)]

    order = (4, -3, 3, -2, 2, -1, 1, 0)

    def block(turn, which):
        to = ((z + order[turn] + Z) % Z) * 2 + which
        at_row = pl.multiple_of(to * DK, DK)
        total = None
        for p in range(3):
            weight = wgt[p, pl.ds(at_row, DK), :]
            for half in grads[p]:
                term = dot(half, weight, 1, 1)
                total = term if total is None else total + term
        return total

    def core_copy(turn):
        return pltpu.make_async_remote_copy(
            src_ref=core_out.at[turn], dst_ref=core_in.at[turn], send_sem=c_s.at[turn],
            recv_sem=c_r.at[turn], device_id=at(dc=1), device_id_type=MESH,
        )

    for turn in range(Z):
        core_out[turn] = block(turn, 1 - core).astype(BF16)
        core_copy(turn).start()

    def z_copy(step, up):
        src, dst, ss, rs = (up_out, up_in, zu_s, zu_r) if up else (dn_out, dn_in, zd_s, zd_r)
        return pltpu.make_async_remote_copy(
            src_ref=src.at[step], dst_ref=dst.at[step], send_sem=ss.at[step], recv_sem=rs.at[step],
            device_id=at(dz=1) if up else at(dz=-1), device_id_type=MESH,
        )

    for turn in range(Z):
        own[turn] = block(turn, core)
    for turn in range(Z):
        core_copy(turn).wait_recv()
        mine = own[turn] + core_in[turn].astype(F32)
        step, up = turn // 2, turn % 2 == 0
        if turn == Z - 1:
            z_copy(3, True).wait_recv()
            z_copy(2, False).wait_recv()
            mine = mine + up_in[3].astype(F32) + dn_in[2].astype(F32)
            out[...] = mine.astype(BF16)
            continue
        if step > 0:
            z_copy(step - 1, up).wait_recv()
            mine = mine + (up_in if up else dn_in)[step - 1].astype(F32)
        (up_out if up else dn_out)[step] = mine.astype(BF16)
        z_copy(step, up).start()

    for step in range(4):
        for piece in range(3):
            y_copy(step, piece, True).wait_send()
            if step < 3:
                y_copy(step, piece, False).wait_send()
        z_copy(step, True).wait_send()
        if step < 3:
            z_copy(step, False).wait_send()
    for copy in x_copies:
        copy.wait_send()
    for turn in range(Z):
        core_copy(turn).wait_send()


def on_device(tokens, qkv_weight, beta_logit, log_decay, out_grad):
    dma = pltpu.SemaphoreType.DMA
    return pl.pallas_call(
        kernel,
        out_shape=jax.ShapeDtypeStruct((C, DK), BF16),
        in_specs=[pl.BlockSpec(memory_space=pltpu.VMEM)] * 5,
        out_specs=pl.BlockSpec(memory_space=pltpu.VMEM),
        scratch_shapes=[
            pltpu.VMEM((Y, ROWS, DK), BF16),
            pltpu.VMEM((X, ROWS, DK), BF16),
            pltpu.VMEM((3, DK, 2 * DK), F32),
            pltpu.VMEM((Z, C, DK), BF16),
            pltpu.VMEM((Z, C, DK), BF16),
            pltpu.VMEM((Z, C, DK), F32),
            pltpu.VMEM((4, C, DK), BF16),
            pltpu.VMEM((3, C, DK), BF16),
            pltpu.VMEM((4, C, DK), BF16),
            pltpu.VMEM((3, C, DK), BF16),
            pltpu.VMEM((2, DK, DK), F32),
            dma((4, 3)), dma((4, 3)), dma((3, 3)), dma((3, 3)),
            dma((X,)), dma((X,)),
            dma((Z,)), dma((Z,)),
            dma((4,)), dma((4,)), dma((3,)), dma((3,)),
        ],
        compiler_params=pltpu.CompilerParams(
            collective_id=0, has_side_effects=True, vmem_limit_bytes=40 * 2**20
        ),
        name="delta_rule",
    )(tokens, qkv_weight, beta_logit, log_decay, out_grad)


def solution(mesh):
    return jax.shard_map(
        on_device,
        mesh=mesh,
        in_specs=(
            P("seq", None),
            P(None, None, "head"),
            P("head", "seq"),
            P("head", "seq"),
            P("seq", "head"),
        ),
        out_specs=P("seq", "head"),
        check_vma=False,
    )
```

```python
import functools

import jax
import jax.numpy as jnp
from jax import lax
from jax.experimental import pallas as pl
from jax.experimental.pallas import tpu as pltpu
from jax.sharding import PartitionSpec as P

F32 = jnp.float32
BF16 = jnp.bfloat16
MESH = pl.DeviceIdType.MESH
X, Y, Z = 4, 8, 8
C, DK = 256, 128
B_AT, R_AT, A_AT, Z_AT, ROWS = 0, 128, 256, 272, 400
PIECES = ((R_AT, 144), (B_AT, 128), (Z_AT, 128))
FAR = ((0, 208), (208, 192))
K_PARTS, K_PART = 4, 512
HALVES, H_ROWS = 2, 128


def dot(a, b, ca=1, cb=0):
    return lax.dot_general(
        a.astype(BF16), b.astype(BF16), (((ca,), (cb,)), ((), ())), preferred_element_type=F32
    )


def split(a):
    upper = a.astype(BF16)
    return upper, (a - upper.astype(F32)).astype(BF16)


def thirds(a):
    upper, rest = split(a)
    middle = rest
    lower = (a - upper.astype(F32) - middle.astype(F32)).astype(BF16)
    return upper, middle, lower


def unit_inverse_less_identity(low, rows, cols):
    def same(shift):
        return (rows >> shift) == (cols >> shift)

    power = jnp.where(same(5), low, 0.0)
    off = -power
    for _ in range(4):
        power = dot(power, power)
        off = off + power + dot(off, power)
    for shift in (5, 6, 7):
        inside = jnp.where(same(shift + 1) & ~same(shift), low, 0.0)
        left = inside + dot(off, inside)
        off = off - left - dot(left, off)
    return off


def kernel(
    tok_hbm, wgt_hbm, bl_hbm, ld_hbm, og_hbm, out,
    tok, wgt, bl, ld, og, ag, xg, core_out, core_in, own, up_out, dn_out, up_in, dn_in,
    in_sem, w_sem, up_s, up_r, dn_s, dn_r, far_s, far_r, x_s, x_r, c_s, c_r, zu_s, zu_r, zd_s, zd_r,
):
    seq, head = lax.axis_index("seq"), lax.axis_index("head")
    x, y = seq // Y, seq % Y
    z, core = head // 2, head % 2

    def at(dx=0, dy=0, dz=0, dc=0):
        return (
            ((x + dx) % X) * Y + (y + dy + Y) % Y,
            ((z + dz + Z) % Z) * 2 + (core + dc) % 2,
        )

    small = [
        pltpu.make_async_copy(src, dst, in_sem.at[i])
        for i, (src, dst) in enumerate(((ld_hbm, ld), (bl_hbm, bl), (og_hbm, og)))
    ]
    parts = []
    for k in range(K_PARTS):
        rows_k = pl.ds(k * K_PART, K_PART)
        parts.append(
            [pltpu.make_async_copy(tok_hbm.at[:, rows_k], tok.at[:, rows_k], in_sem.at[3 + k])]
            + [
                pltpu.make_async_copy(
                    wgt_hbm.at[p, rows_k, :], wgt.at[rows_k, pl.ds(p * DK, DK)], w_sem.at[k, p]
                )
                for p in range(3)
            ]
        )
    for copy in small[:2] + sum(parts, []) + small[2:]:
        copy.start()
    peers = [at(dy=1), at(dy=-1), at(dx=1), at(dx=2), at(dx=3), at(dc=1), at(dz=1), at(dz=-1)]
    barrier = pltpu.get_barrier_semaphore()
    for peer in peers:
        pl.semaphore_signal(barrier, inc=1, device_id=peer, device_id_type=MESH)

    rows = lax.broadcasted_iota(jnp.int32, (C, C), 0)
    cols = lax.broadcasted_iota(jnp.int32, (C, C), 1)
    causal, anti = rows >= cols, rows <= cols
    small[0].wait()
    small[1].wait()
    beta_row = 1.0 / (1.0 + jnp.exp(-bl[...]))
    beta = jnp.sum(jnp.where(rows == cols, beta_row, 0.0), axis=1, keepdims=True)
    cum = jnp.sum(jnp.where(cols <= rows, ld[...], 0.0), axis=1, keepdims=True)
    cum_row = jnp.sum(jnp.where(rows == cols, cum, 0.0), axis=0, keepdims=True)
    total = cum[C - 1 : C, :]
    decay = jnp.exp(-jnp.abs(cum - cum_row))
    opening = jnp.exp(cum)
    fading = jnp.exp(total - cum)

    proj = None
    for k in range(K_PARTS):
        for copy in parts[k]:
            copy.wait()
        rows_k = pl.ds(k * K_PART, K_PART)
        term = jnp.dot(tok[:, rows_k], wgt[rows_k, :], preferred_element_type=F32)
        proj = term if proj is None else proj + term
    small[2].wait()
    q, key, v = proj[:, :DK], proj[:, DK : 2 * DK], proj[:, 2 * DK :]
    q_inv = lax.rsqrt(jnp.sum(q * q, axis=1, keepdims=True) + 1e-6)
    k_inv = lax.rsqrt(jnp.sum(key * key, axis=1, keepdims=True) + 1e-6)
    qn, kn = q * q_inv, key * k_inv
    g = og[...]

    kb = kn.astype(BF16)
    qb = qn.astype(BF16)
    low = beta * jnp.where(rows > cols, decay * dot(kb, kb, 1, 1), 0.0)
    off = unit_inverse_less_identity(low, rows, cols).astype(BF16)
    bk = opening * kn
    fk = fading * kn
    x0 = beta * bk
    xs = x0 + dot(off, x0)
    xf = beta * (fk + dot(off, fk, 0, 0))
    v0 = beta * v
    w0 = v0 + dot(off, v0)
    pg = dot(jnp.where(anti, decay * dot(kb, qb, 1, 1), 0.0), g)
    y0 = beta * (pg + dot(off, pg, 0, 0))
    fk_hi, fk_lo = split(fk)
    w_hi, w_lo = split(w0)
    b_seg = dot(fk_hi, w_hi, 0, 0) + (dot(fk_lo, w_hi, 0, 0) + dot(fk_hi, w_lo, 0, 0))
    z_seg = dot(opening * qn, g, 0, 0) - dot(xs, pg, 0, 0)
    r_seg = -dot(xf, bk, 0, 0)
    a_seg = jnp.broadcast_to(jnp.exp(total), (1, DK))

    def put(ref, a, r, b, zz):
        ref[pl.ds(B_AT, DK), :] = b.astype(BF16)
        ref[pl.ds(R_AT, DK), :] = r.astype(BF16)
        ref[pl.ds(Z_AT, DK), :] = zz.astype(BF16)
        place = lax.broadcasted_iota(jnp.int32, (16, DK), 0)
        first, second, third = [t.astype(F32) for t in thirds(a)]
        tile = jnp.where(place == 0, first, jnp.where(place == 1, second, jnp.where(place == 2, third, 0.0)))
        ref[pl.ds(A_AT, 16), :] = tile.astype(BF16)

    def scale_of(ref):
        return jnp.sum(ref[pl.ds(A_AT, 16), :].astype(F32), axis=0, keepdims=True)

    put(ag.at[y], a_seg, r_seg, b_seg, z_seg)
    pl.semaphore_wait(barrier, len(peers))

    def y_copy(step, piece, up):
        slot = (y - step + Y) % Y if up else (y + step) % Y
        if step < 3:
            start, size = PIECES[piece]
            ss, rs = (up_s, up_r) if up else (dn_s, dn_r)
            ss, rs = ss.at[step, piece], rs.at[step, piece]
        else:
            start, size = FAR[0 if up else 1]
            ss, rs = far_s.at[0 if up else 1], far_r.at[0 if up else 1]
        part = ag.at[slot, pl.ds(start, size)]
        return pltpu.make_async_remote_copy(
            src_ref=part, dst_ref=part, send_sem=ss, recv_sem=rs,
            device_id=at(dy=1) if up else at(dy=-1), device_id_type=MESH,
        )

    def y_arrived(step, piece, up):
        slot = (y - step - 1 + Y) % Y if up else (y + step + 1) % Y
        if step < 3:
            start, size = PIECES[piece]
            ss, rs = (up_s, up_r) if up else (dn_s, dn_r)
            ss, rs = ss.at[step, piece], rs.at[step, piece]
        else:
            start, size = FAR[0 if up else 1]
            ss, rs = far_s.at[0 if up else 1], far_r.at[0 if up else 1]
        part = ag.at[slot, pl.ds(start, size)]
        pltpu.make_async_remote_copy(
            src_ref=part, dst_ref=part, send_sem=ss, recv_sem=rs,
            device_id=at(dy=1) if up else at(dy=-1), device_id_type=MESH,
        ).wait_recv()

    for step in range(4):
        for piece in range(3):
            for up in (True, False):
                if step > 0:
                    y_arrived(step - 1, piece, up)
                if step < 3:
                    y_copy(step, piece, up).start()
                elif piece == (1 if up else 2):
                    y_copy(3, 0, up).start()
    y_arrived(3, 0, True)
    y_arrived(3, 0, False)

    def leaf(slot):
        r = ag[slot, pl.ds(R_AT, DK), :].astype(F32)
        return (
            scale_of(ag.at[slot]), r, r.T,
            ag[slot, pl.ds(B_AT, DK), :].astype(F32), ag[slot, pl.ds(Z_AT, DK), :].astype(F32),
        )

    def wide(left, right):
        return jnp.concatenate([left, right], axis=1)

    def ahead(early, late):
        a0, r0, _, b0, _ = early
        a1, r1, _, b1, _ = late
        both = dot(r1, wide(r0, b0))
        return a0 * a1, a1 * r0 + a0 * r1 + both[:, :DK], a1 * b0 + b1 + both[:, DK:]

    def behind(early, late):
        a0, _, t0, _, z0 = early
        a1, _, t1, _, z1 = late
        both = dot(t0, wide(t1, z1))
        return a0 * a1, a1 * t0 + a0 * t1 + both[:, :DK], a0 * z1 + z0 + both[:, DK:]

    def compose(early, late):
        a, r, b = ahead(early, late)
        _, t, zz = behind(early, late)
        return a, r, t, b, zz

    def pick(flag, one, other):
        return tuple(jnp.where(flag, p, o) for p, o in zip(one, other))

    leaves = [leaf(j) for j in range(Y)]
    pairs = [compose(leaves[2 * j], leaves[2 * j + 1]) for j in range(4)]
    quads = [compose(pairs[0], pairs[1]), compose(pairs[2], pairs[3])]
    a_row, r_row, b_row = ahead(quads[0], quads[1])
    _, _, z_row = behind(quads[0], quads[1])

    put(xg.at[x], a_row, r_row, b_row, z_row)
    x_copies = []
    for m in (2, 1, 3):
        start = pl.multiple_of(jnp.where(x + m < X, B_AT, R_AT), 128)
        part = xg.at[x, pl.ds(start, 272)]
        x_copies.append(
            pltpu.make_async_remote_copy(
                src_ref=part, dst_ref=part, send_sem=x_s.at[m], recv_sem=x_r.at[m],
                device_id=at(dx=m), device_id_type=MESH,
            )
        )
        x_copies[-1].start()

    zero = jnp.zeros((DK, DK), F32)
    none = (jnp.ones((1, DK), F32), zero, zero, zero, zero)
    four, two, one = y >= 4, y % 4 >= 2, y % 2 == 1
    before = pick(four, quads[0], none)
    second = pick(two, pick(four, pairs[2], pairs[0]), none)
    third = pick(one, leaf(y - y % 2), none)
    a_pre, r_pre, b_pre = ahead(before, second)
    a_pre, r_pre, b_pre = ahead((a_pre, r_pre, None, b_pre, None), third)
    first = pick(one, none, leaf(y + 1 - y % 2))
    second = pick(two, none, pick(four, pairs[3], pairs[1]))
    last = pick(four, none, quads[1])
    a_suf, t_suf, z_suf = behind(second, last)
    a_suf, t_suf, z_suf = behind(first, (a_suf, None, t_suf, None, z_suf))

    for m in (1, 3, 2):
        source = (x - m + X) % X
        start = pl.multiple_of(jnp.where(source < x, B_AT, R_AT), 128)
        part = xg.at[source, pl.ds(start, 272)]
        pltpu.make_async_remote_copy(
            src_ref=part, dst_ref=part, send_sem=x_s.at[m], recv_sem=x_r.at[m],
            device_id=at(dx=m), device_id_type=MESH,
        ).wait_recv()
    state, seed = zero, zero
    for j in range(X - 1):
        i = X - 1 - j
        r_j, r_i = xg[j, pl.ds(R_AT, DK), :], xg[i, pl.ds(R_AT, DK), :]
        grown = xg[j, pl.ds(B_AT, DK), :].astype(F32)
        if j:
            grown = grown + scale_of(xg.at[j]) * state + dot(r_j, state)
        state = jnp.where(j < x, grown, state)
        grown = xg[i, pl.ds(Z_AT, DK), :].astype(F32)
        if j:
            grown = grown + scale_of(xg.at[i]) * seed + dot(r_i, seed, 0, 0)
        seed = jnp.where(i > x, grown, seed)
    s_in = a_pre * state + dot(r_pre, state) + b_pre
    g_out = a_suf * seed + dot(t_suf, seed) + z_suf

    w = w0 - dot(xs, s_in)
    yy = y0 + dot(xf, g_out)
    wb, yb = w.astype(BF16), yy.astype(BF16)
    s_hi, s_lo = split(s_in)
    e = jnp.where(causal, decay * dot(g, wb, 1, 1), 0.0)
    et = jnp.where(anti, decay * dot(wb, g, 1, 1), 0.0)
    h = jnp.where(rows > cols, dot(yb, wb, 1, 1), dot(wb, yb, 1, 1)) * decay
    h = jnp.where(rows == cols, 0.0, h)
    dq = opening * (dot(g, s_hi, 1, 1) + dot(g, s_lo, 1, 1)) + dot(e, kb)
    dk = fading * dot(wb, g_out, 1, 1) + dot(et, qb) - dot(h, kb) - opening * dot(yb, s_hi, 1, 1)
    dq = q_inv * (dq - qn * jnp.sum(qn * dq, axis=1, keepdims=True))
    dk = k_inv * (dk - kn * jnp.sum(kn * dk, axis=1, keepdims=True))
    grads_hi, grads_lo = split(jnp.concatenate([dq, dk, yy], axis=1))

    order = (4, -3, 3, -2, 2, -1, 1, 0)

    def core_copy(turn):
        return pltpu.make_async_remote_copy(
            src_ref=core_out.at[turn], dst_ref=core_in.at[turn], send_sem=c_s.at[turn],
            recv_sem=c_r.at[turn], device_id=at(dc=1), device_id_type=MESH,
        )

    def product(turn):
        to = pl.multiple_of(((z + order[turn] + Z) % Z) * 2 * DK, 2 * DK)
        weight = wgt[pl.ds(to, 2 * DK), :]
        both = dot(grads_hi, weight, 1, 1) + dot(grads_lo, weight, 1, 1)
        left, right = both[:, :DK], both[:, DK:]
        core_out[turn] = jnp.where(core == 0, right, left).astype(BF16)
        core_copy(turn).start()
        own[turn] = jnp.where(core == 0, left, right)

    def z_copy(step, half, up):
        src, dst, ss, rs = (up_out, up_in, zu_s, zu_r) if up else (dn_out, dn_in, zd_s, zd_r)
        part = pl.ds(half * H_ROWS, H_ROWS)
        return pltpu.make_async_remote_copy(
            src_ref=src.at[step, part], dst_ref=dst.at[step, part], send_sem=ss.at[step, half],
            recv_sem=rs.at[step, half], device_id=at(dz=1) if up else at(dz=-1), device_id_type=MESH,
        )

    def pass_on(step):
        turns = [(2 * step, True)] + ([(2 * step + 1, False)] if step < 3 else [])
        for turn, up in turns:
            core_copy(turn).wait_recv()
        for half in range(HALVES):
            part = pl.ds(half * H_ROWS, H_ROWS)
            for turn, up in turns:
                mine = own[turn, part, :] + core_in[turn, part, :].astype(F32)
                if step:
                    z_copy(step - 1, half, up).wait_recv()
                    mine = mine + (up_in if up else dn_in)[step - 1, part, :].astype(F32)
                (up_out if up else dn_out)[step, part, :] = mine.astype(BF16)
                z_copy(step, half, up).start()

    for turn in range(4):
        product(turn)
    pass_on(0)
    for turn in range(4, Z):
        product(turn)
    for step in range(1, 4):
        pass_on(step)
    core_copy(Z - 1).wait_recv()
    for half in range(HALVES):
        part = pl.ds(half * H_ROWS, H_ROWS)
        mine = own[Z - 1, part, :] + core_in[Z - 1, part, :].astype(F32)
        z_copy(2, half, False).wait_recv()
        mine = mine + dn_in[2, part, :].astype(F32)
        z_copy(3, half, True).wait_recv()
        out[part, :] = (mine + up_in[3, part, :].astype(F32)).astype(BF16)

    for step in range(4):
        for piece in range(3 if step < 3 else 1):
            y_copy(step, piece, True).wait_send()
            y_copy(step, piece, False).wait_send()
        for half in range(HALVES):
            z_copy(step, half, True).wait_send()
            if step < 3:
                z_copy(step, half, False).wait_send()
    for copy in x_copies:
        copy.wait_send()
    for turn in range(Z):
        core_copy(turn).wait_send()


def on_device(tokens, qkv_weight, beta_logit, log_decay, out_grad):
    dma = pltpu.SemaphoreType.DMA
    return pl.pallas_call(
        kernel,
        out_shape=jax.ShapeDtypeStruct((C, DK), BF16),
        in_specs=[pl.BlockSpec(memory_space=pl.ANY)] * 5,
        out_specs=pl.BlockSpec(memory_space=pltpu.VMEM),
        scratch_shapes=[
            pltpu.VMEM((C, K_PARTS * K_PART), BF16),
            pltpu.VMEM((K_PARTS * K_PART, 3 * DK), BF16),
            pltpu.VMEM((1, C), F32),
            pltpu.VMEM((1, C), F32),
            pltpu.VMEM((C, DK), BF16),
            pltpu.VMEM((Y, ROWS, DK), BF16),
            pltpu.VMEM((X, ROWS, DK), BF16),
            pltpu.VMEM((Z, C, DK), BF16),
            pltpu.VMEM((Z, C, DK), BF16),
            pltpu.VMEM((Z, C, DK), F32),
            pltpu.VMEM((4, C, DK), BF16),
            pltpu.VMEM((3, C, DK), BF16),
            pltpu.VMEM((4, C, DK), BF16),
            pltpu.VMEM((3, C, DK), BF16),
            dma((3 + K_PARTS,)), dma((K_PARTS, 3)),
            dma((3, 3)), dma((3, 3)), dma((3, 3)), dma((3, 3)), dma((2,)), dma((2,)),
            dma((X,)), dma((X,)),
            dma((Z,)), dma((Z,)),
            dma((4, HALVES)), dma((4, HALVES)), dma((3, HALVES)), dma((3, HALVES)),
        ],
        compiler_params=pltpu.CompilerParams(
            collective_id=0, has_side_effects=True, vmem_limit_bytes=63 * 2**20
        ),
        name="delta_rule",
    )(tokens, qkv_weight, beta_logit, log_decay, out_grad)


def solution(mesh):
    return jax.shard_map(
        on_device,
        mesh=mesh,
        in_specs=(
            P("seq", None),
            P(None, None, "head"),
            P("head", "seq"),
            P("head", "seq"),
            P("seq", "head"),
        ),
        out_specs=P("seq", "head"),
        check_vma=False,
    )
```

```python
import functools

import jax
import jax.numpy as jnp
from jax import lax
from jax.experimental import pallas as pl
from jax.experimental.pallas import tpu as pltpu
from jax.sharding import PartitionSpec as P

F32 = jnp.float32
BF16 = jnp.bfloat16
MESH = pl.DeviceIdType.MESH
X, Y, Z = 4, 8, 8
C, DK = 256, 128
B_AT, R_AT, A_AT, Z_AT, ROWS = 0, 128, 256, 272, 400
PIECES = ((R_AT, 144), (B_AT, 128), (Z_AT, 128))
K_PARTS, K_PART = 2, 1024
ORDER = (4, -3, 3, -2, 2, -1, 1, 0)
LAG = 3


def dot(a, b, ca=1, cb=0):
    return lax.dot_general(
        a.astype(BF16), b.astype(BF16), (((ca,), (cb,)), ((), ())), preferred_element_type=F32
    )


def split(a):
    upper = a.astype(BF16)
    return upper, (a - upper.astype(F32)).astype(BF16)


def thirds(a):
    upper, rest = split(a)
    middle = rest
    lower = (a - upper.astype(F32) - middle.astype(F32)).astype(BF16)
    return upper, middle, lower


def unit_inverse_less_identity(low, rows, cols):
    def same(shift):
        return (rows >> shift) == (cols >> shift)

    power = jnp.where(same(5), low, 0.0)
    off = -power
    for _ in range(4):
        power = dot(power, power)
        off = off + power + dot(off, power)
    for shift in (5, 6, 7):
        inside = jnp.where(same(shift + 1) & ~same(shift), low, 0.0)
        left = inside + dot(off, inside)
        off = off - left - dot(left, off)
    return off


def kernel(
    tok_hbm, wgt_hbm, bl_hbm, ld_hbm, og_hbm, out,
    tok, wgt, bl, ld, og, ag, qg, xg, core_out, core_in, own, z_out, z_in,
    in_sem, w_sem, a_s, a_r, q_s, q_r, x_s, x_r, c_s, c_r, z_s, z_r,
):
    seq, head = lax.axis_index("seq"), lax.axis_index("head")
    x, y = seq // Y, seq % Y
    z, core = head // 2, head % 2

    def at(dx=0, dy=0, dz=0, dc=0):
        return (
            ((x + dx) % X) * Y + (y + dy + Y) % Y,
            ((z + dz + Z) % Z) * 2 + (core + dc) % 2,
        )

    small = [
        pltpu.make_async_copy(src, dst, in_sem.at[i])
        for i, (src, dst) in enumerate(((ld_hbm, ld), (bl_hbm, bl), (og_hbm, og)))
    ]
    parts = []
    for k in range(K_PARTS):
        rows_k = pl.ds(k * K_PART, K_PART)
        parts.append(
            [pltpu.make_async_copy(tok_hbm.at[:, rows_k], tok.at[:, rows_k], in_sem.at[3 + k])]
            + [
                pltpu.make_async_copy(
                    wgt_hbm.at[p, rows_k, :], wgt.at[p, rows_k, :], w_sem.at[k, p]
                )
                for p in range(3)
            ]
        )
    for copy in small[:2] + sum(parts, []) + small[2:]:
        copy.start()
    pair, odd = y // 2, y % 2
    way = 2 * odd - 1
    peers = [at(dy=m * way) for m in (-2, -1, 1, 2, 3)]
    peers += [at(dx=m) for m in (1, 2, 3)] + [at(dc=1)] + [at(dz=m) for m in range(1, Z)]
    barrier = pltpu.get_barrier_semaphore()
    for peer in peers:
        pl.semaphore_signal(barrier, inc=1, device_id=peer, device_id_type=MESH)

    rows = lax.broadcasted_iota(jnp.int32, (C, C), 0)
    cols = lax.broadcasted_iota(jnp.int32, (C, C), 1)
    causal, anti = rows >= cols, rows <= cols
    small[0].wait()
    small[1].wait()
    beta_row = 1.0 / (1.0 + jnp.exp(-bl[...]))
    beta = jnp.sum(jnp.where(rows == cols, beta_row, 0.0), axis=1, keepdims=True)
    cum = jnp.sum(jnp.where(cols <= rows, ld[...], 0.0), axis=1, keepdims=True)
    cum_row = jnp.sum(jnp.where(rows == cols, cum, 0.0), axis=0, keepdims=True)
    total = cum[C - 1 : C, :]
    decay = jnp.exp(-jnp.abs(cum - cum_row))
    opening = jnp.exp(cum)
    fading = jnp.exp(total - cum)

    def weights(at_rows):
        return jnp.concatenate([wgt[p, at_rows, :] for p in range(3)], axis=1)

    proj = None
    for k in range(K_PARTS):
        for copy in parts[k]:
            copy.wait()
        rows_k = pl.ds(k * K_PART, K_PART)
        term = jnp.dot(tok[:, rows_k], weights(rows_k), preferred_element_type=F32)
        proj = term if proj is None else proj + term
    small[2].wait()
    q, key, v = proj[:, :DK], proj[:, DK : 2 * DK], proj[:, 2 * DK :]
    q_inv = lax.rsqrt(jnp.sum(q * q, axis=1, keepdims=True) + 1e-6)
    k_inv = lax.rsqrt(jnp.sum(key * key, axis=1, keepdims=True) + 1e-6)
    qn, kn = q * q_inv, key * k_inv
    g = og[...]

    kb = kn.astype(BF16)
    qb = qn.astype(BF16)
    low = beta * jnp.where(rows > cols, decay * dot(kb, kb, 1, 1), 0.0)
    off = unit_inverse_less_identity(low, rows, cols).astype(BF16)
    bk = opening * kn
    fk = fading * kn
    x0 = beta * bk
    xs = x0 + dot(off, x0)
    xf = beta * (fk + dot(off, fk, 0, 0))
    r_seg = -dot(xf, bk, 0, 0)
    a_seg = jnp.broadcast_to(jnp.exp(total), (1, DK))

    def put_r(ref, a, r):
        ref[pl.ds(R_AT, DK), :] = r.astype(BF16)
        place = lax.broadcasted_iota(jnp.int32, (16, DK), 0)
        first, second, third = [t.astype(F32) for t in thirds(a)]
        tile = jnp.where(place == 0, first, jnp.where(place == 1, second, jnp.where(place == 2, third, 0.0)))
        ref[pl.ds(A_AT, 16), :] = tile.astype(BF16)

    def put(ref, a, r, b, zz):
        put_r(ref, a, r)
        ref[pl.ds(B_AT, DK), :] = b.astype(BF16)
        ref[pl.ds(Z_AT, DK), :] = zz.astype(BF16)

    def scale_of(ref):
        return jnp.sum(ref[pl.ds(A_AT, 16), :].astype(F32), axis=0, keepdims=True)

    def pair_copy(piece, slot):
        start, size = PIECES[piece]
        part = ag.at[slot, pl.ds(start, size)]
        return pltpu.make_async_remote_copy(
            src_ref=part, dst_ref=part, send_sem=a_s.at[piece], recv_sem=a_r.at[piece],
            device_id=at(dy=-way), device_id_type=MESH,
        )

    put_r(ag.at[odd], a_seg, r_seg)
    pl.semaphore_wait(barrier, len(peers))
    pair_copy(0, odd).start()
    v0 = beta * v
    w0 = v0 + dot(off, v0)
    fk_hi, fk_lo = split(fk)
    w_hi, w_lo = split(w0)
    b_seg = dot(fk_hi, w_hi, 0, 0) + (dot(fk_lo, w_hi, 0, 0) + dot(fk_hi, w_lo, 0, 0))
    ag[odd, pl.ds(B_AT, DK), :] = b_seg.astype(BF16)
    pair_copy(1, odd).start()
    pg = dot(jnp.where(anti, decay * dot(kb, qb, 1, 1), 0.0), g)
    z_seg = dot(opening * qn, g, 0, 0) - dot(xs, pg, 0, 0)
    ag[odd, pl.ds(Z_AT, DK), :] = z_seg.astype(BF16)
    pair_copy(2, odd).start()
    y0 = beta * (pg + dot(off, pg, 0, 0))

    def leaf(ref):
        r = ref[pl.ds(R_AT, DK), :].astype(F32)
        return (
            scale_of(ref), r, r.T, ref[pl.ds(B_AT, DK), :].astype(F32), ref[pl.ds(Z_AT, DK), :].astype(F32)
        )

    def wide(left, right):
        return jnp.concatenate([left, right], axis=1)

    def ahead(early, late):
        a0, r0, _, b0, _ = early
        a1, r1, _, b1, _ = late
        both = dot(r1, wide(r0, b0))
        return a0 * a1, a1 * r0 + a0 * r1 + both[:, :DK], a1 * b0 + b1 + both[:, DK:]

    def behind(early, late):
        a0, _, t0, _, z0 = early
        a1, _, t1, _, z1 = late
        both = dot(t0, wide(t1, z1))
        return a0 * a1, a1 * t0 + a0 * t1 + both[:, :DK], a0 * z1 + z0 + both[:, DK:]

    def compose(early, late):
        a, r, b = ahead(early, late)
        _, t, zz = behind(early, late)
        return a, r, t, b, zz

    def pick(flag, one, other):
        return tuple(jnp.where(flag, p, o) for p, o in zip(one, other))

    for piece in range(3):
        pair_copy(piece, 1 - odd).wait_recv()
    early, late = leaf(ag.at[0]), leaf(ag.at[1])
    a_pair, r_pair, b_pair = ahead(early, late)
    _, _, z_pair = behind(early, late)

    put(qg.at[pair], a_pair, r_pair, b_pair, z_pair)

    def row_copy(m, slot):
        part = qg.at[slot]
        return pltpu.make_async_remote_copy(
            src_ref=part, dst_ref=part, send_sem=q_s.at[m], recv_sem=q_r.at[m],
            device_id=at(dy=m * way), device_id_type=MESH,
        )

    for m in (3, 2, 1):
        row_copy(m, pair).start()
    for m, shift in ((1, way), (2, -way), (3, 2)):
        row_copy(m, (pair + shift + 4) % 4).wait_recv()
    pairs = [leaf(qg.at[j]) for j in range(4)]
    quads = [compose(pairs[0], pairs[1]), compose(pairs[2], pairs[3])]
    a_row, r_row, b_row = ahead(quads[0], quads[1])
    _, _, z_row = behind(quads[0], quads[1])

    put(xg.at[x], a_row, r_row, b_row, z_row)
    x_copies = []
    for m in (2, 1, 3):
        start = pl.multiple_of(jnp.where(x + m < X, B_AT, R_AT), 128)
        part = xg.at[x, pl.ds(start, 272)]
        x_copies.append(
            pltpu.make_async_remote_copy(
                src_ref=part, dst_ref=part, send_sem=x_s.at[m], recv_sem=x_r.at[m],
                device_id=at(dx=m), device_id_type=MESH,
            )
        )
        x_copies[-1].start()

    zero = jnp.zeros((DK, DK), F32)
    none = (jnp.ones((1, DK), F32), zero, zero, zero, zero)
    four, two, one = y >= 4, y % 4 >= 2, y % 2 == 1
    before = pick(four, quads[0], none)
    second = pick(two, pick(four, pairs[2], pairs[0]), none)
    third = pick(one, early, none)
    a_pre, r_pre, b_pre = ahead(before, second)
    a_pre, r_pre, b_pre = ahead((a_pre, r_pre, None, b_pre, None), third)
    first = pick(one, none, late)
    second = pick(two, none, pick(four, pairs[3], pairs[1]))
    last = pick(four, none, quads[1])
    a_suf, t_suf, z_suf = behind(second, last)
    a_suf, t_suf, z_suf = behind(first, (a_suf, None, t_suf, None, z_suf))

    for m in (1, 3, 2):
        source = (x - m + X) % X
        start = pl.multiple_of(jnp.where(source < x, B_AT, R_AT), 128)
        part = xg.at[source, pl.ds(start, 272)]
        pltpu.make_async_remote_copy(
            src_ref=part, dst_ref=part, send_sem=x_s.at[m], recv_sem=x_r.at[m],
            device_id=at(dx=m), device_id_type=MESH,
        ).wait_recv()
    state, seed = zero, zero
    for j in range(X - 1):
        i = X - 1 - j
        r_j, r_i = xg[j, pl.ds(R_AT, DK), :], xg[i, pl.ds(R_AT, DK), :]
        grown = xg[j, pl.ds(B_AT, DK), :].astype(F32)
        if j:
            grown = grown + scale_of(xg.at[j]) * state + dot(r_j, state)
        state = jnp.where(j < x, grown, state)
        grown = xg[i, pl.ds(Z_AT, DK), :].astype(F32)
        if j:
            grown = grown + scale_of(xg.at[i]) * seed + dot(r_i, seed, 0, 0)
        seed = jnp.where(i > x, grown, seed)
    s_in = a_pre * state + dot(r_pre, state) + b_pre
    g_out = a_suf * seed + dot(t_suf, seed) + z_suf

    w = w0 - dot(xs, s_in)
    yy = y0 + dot(xf, g_out)
    wb, yb = w.astype(BF16), yy.astype(BF16)
    s_hi, s_lo = split(s_in)
    e = jnp.where(causal, decay * dot(g, wb, 1, 1), 0.0)
    et = jnp.where(anti, decay * dot(wb, g, 1, 1), 0.0)
    h = jnp.where(rows > cols, dot(yb, wb, 1, 1), dot(wb, yb, 1, 1)) * decay
    h = jnp.where(rows == cols, 0.0, h)
    dq = opening * (dot(g, s_hi, 1, 1) + dot(g, s_lo, 1, 1)) + dot(e, kb)
    dk = fading * dot(wb, g_out, 1, 1) + dot(et, qb) - dot(h, kb) - opening * dot(yb, s_hi, 1, 1)
    dq = q_inv * (dq - qn * jnp.sum(qn * dq, axis=1, keepdims=True))
    dk = k_inv * (dk - kn * jnp.sum(kn * dk, axis=1, keepdims=True))
    grads_hi, grads_lo = split(jnp.concatenate([dq, dk, yy], axis=1))

    def core_copy(turn):
        return pltpu.make_async_remote_copy(
            src_ref=core_out.at[turn], dst_ref=core_in.at[turn], send_sem=c_s.at[turn],
            recv_sem=c_r.at[turn], device_id=at(dc=1), device_id_type=MESH,
        )

    def z_copy(turn):
        return pltpu.make_async_remote_copy(
            src_ref=z_out.at[turn], dst_ref=z_in.at[turn], send_sem=z_s.at[turn],
            recv_sem=z_r.at[turn], device_id=at(dz=ORDER[turn]), device_id_type=MESH,
        )

    def product(turn):
        to = pl.multiple_of(((z + ORDER[turn] + Z) % Z) * 2 * DK, 2 * DK)
        weight = weights(pl.ds(to, 2 * DK))
        both = dot(grads_hi, weight, 1, 1) + dot(grads_lo, weight, 1, 1)
        left, right = both[:, :DK], both[:, DK:]
        core_out[turn] = jnp.where(core == 0, right, left).astype(BF16)
        core_copy(turn).start()
        own[turn] = jnp.where(core == 0, left, right)

    def pass_on(turn):
        core_copy(turn).wait_recv()
        z_out[turn] = (own[turn] + core_in[turn].astype(F32)).astype(BF16)
        z_copy(turn).start()

    for turn in range(Z):
        product(turn)
        if turn >= LAG:
            pass_on(turn - LAG)
    for turn in range(Z - LAG, Z - 1):
        pass_on(turn)
    core_copy(Z - 1).wait_recv()
    mine = own[Z - 1] + core_in[Z - 1].astype(F32)
    for turn in range(Z - 2, -1, -1):
        z_copy(turn).wait_recv()
        mine = mine + z_in[turn].astype(F32)
    out[...] = mine.astype(BF16)

    for piece in range(3):
        pair_copy(piece, odd).wait_send()
    for m in (1, 2, 3):
        row_copy(m, pair).wait_send()
    for copy in x_copies:
        copy.wait_send()
    for turn in range(Z):
        core_copy(turn).wait_send()
        if turn < Z - 1:
            z_copy(turn).wait_send()


def on_device(tokens, qkv_weight, beta_logit, log_decay, out_grad):
    dma = pltpu.SemaphoreType.DMA
    return pl.pallas_call(
        kernel,
        out_shape=jax.ShapeDtypeStruct((C, DK), BF16),
        in_specs=[pl.BlockSpec(memory_space=pl.ANY)] * 5,
        out_specs=pl.BlockSpec(memory_space=pltpu.VMEM),
        scratch_shapes=[
            pltpu.VMEM((C, K_PARTS * K_PART), BF16),
            pltpu.VMEM((3, K_PARTS * K_PART, DK), BF16),
            pltpu.VMEM((1, C), F32),
            pltpu.VMEM((1, C), F32),
            pltpu.VMEM((C, DK), BF16),
            pltpu.VMEM((2, ROWS, DK), BF16),
            pltpu.VMEM((4, ROWS, DK), BF16),
            pltpu.VMEM((X, ROWS, DK), BF16),
            pltpu.VMEM((Z, C, DK), BF16),
            pltpu.VMEM((Z, C, DK), BF16),
            pltpu.VMEM((Z, C, DK), F32),
            pltpu.VMEM((Z - 1, C, DK), BF16),
            pltpu.VMEM((Z - 1, C, DK), BF16),
            dma((3 + K_PARTS,)), dma((K_PARTS, 3)),
            dma((3,)), dma((3,)), dma((4,)), dma((4,)), dma((X,)), dma((X,)),
            dma((Z,)), dma((Z,)), dma((Z - 1,)), dma((Z - 1,)),
        ],
        compiler_params=pltpu.CompilerParams(
            collective_id=0, has_side_effects=True, vmem_limit_bytes=63 * 2**20
        ),
        name="delta_rule",
    )(tokens, qkv_weight, beta_logit, log_decay, out_grad)


def solution(mesh):
    return jax.shard_map(
        on_device,
        mesh=mesh,
        in_specs=(
            P("seq", None),
            P(None, None, "head"),
            P("head", "seq"),
            P("head", "seq"),
            P("seq", "head"),
        ),
        out_specs=P("seq", "head"),
        check_vma=False,
    )
```

```python
import functools

import jax
import jax.numpy as jnp
from jax import lax
from jax.experimental import pallas as pl
from jax.experimental.pallas import tpu as pltpu
from jax.sharding import PartitionSpec as P

F32 = jnp.float32
BF16 = jnp.bfloat16
MESH = pl.DeviceIdType.MESH
X, Y, Z = 4, 8, 8
C, DK = 256, 128
B_AT, R_AT, A_AT, Z_AT, ROWS = 0, 128, 256, 272, 400
PIECES = ((R_AT, 144), (B_AT, 128), (Z_AT, 128))
K_PARTS, K_PART = 2, 1024
ORDER = (4, 3, -3, 1, -1, 2, -2, 0)
HOPS = ((0, 0, 128, 2), (0, 128, 128, -2), (1, 0, 256, 1), (2, 0, 256, -1),
        (3, 0, 256, 1), (4, 0, 256, -1), (5, 0, 256, 2), (6, 0, 256, -2))
LAG = 3


def dot(a, b, ca=1, cb=0):
    return lax.dot_general(
        a.astype(BF16), b.astype(BF16), (((ca,), (cb,)), ((), ())), preferred_element_type=F32
    )


def split(a):
    upper = a.astype(BF16)
    return upper, (a - upper.astype(F32)).astype(BF16)


def thirds(a):
    upper, rest = split(a)
    middle = rest
    lower = (a - upper.astype(F32) - middle.astype(F32)).astype(BF16)
    return upper, middle, lower


def unit_inverse_less_identity(low, rows, cols):
    def same(shift):
        return (rows >> shift) == (cols >> shift)

    power = jnp.where(same(5), low, 0.0)
    off = -power
    for _ in range(4):
        power = dot(power, power)
        off = off + power + dot(off, power)
    for shift in (5, 6, 7):
        inside = jnp.where(same(shift + 1) & ~same(shift), low, 0.0)
        left = inside + dot(off, inside)
        off = off - left - dot(left, off)
    return off


def kernel(
    tok_hbm, wgt_hbm, bl_hbm, ld_hbm, og_hbm, out,
    tok, wgt, bl, ld, og, ag, qg, xg, core_out, core_in, own, z_out, z_in,
    in_sem, w_sem, a_s, a_r, q_s, q_r, x_s, x_r, c_s, c_r, z_s, z_r,
):
    seq, head = lax.axis_index("seq"), lax.axis_index("head")
    x, y = seq // Y, seq % Y
    z, core = head // 2, head % 2

    def at(dx=0, dy=0, dz=0, dc=0):
        return (
            ((x + dx) % X) * Y + (y + dy + Y) % Y,
            ((z + dz + Z) % Z) * 2 + (core + dc) % 2,
        )

    small = [
        pltpu.make_async_copy(src, dst, in_sem.at[i])
        for i, (src, dst) in enumerate(((ld_hbm, ld), (bl_hbm, bl), (og_hbm, og)))
    ]
    parts = []
    for k in range(K_PARTS):
        rows_k = pl.ds(k * K_PART, K_PART)
        parts.append(
            [pltpu.make_async_copy(tok_hbm.at[:, rows_k], tok.at[:, rows_k], in_sem.at[3 + k])]
            + [
                pltpu.make_async_copy(
                    wgt_hbm.at[p, rows_k, :], wgt.at[p, rows_k, :], w_sem.at[k, p]
                )
                for p in range(3)
            ]
        )
    for copy in small[:2] + sum(parts, []) + small[2:]:
        copy.start()
    pair, odd = y // 2, y % 2
    way = 2 * odd - 1
    peers = [at(dy=m * way) for m in (-2, -1, 1, 2, 3)]
    peers += [at(dx=m) for m in (1, 2, 3)] + [at(dc=1)] + [at(dz=m) for m in (-2, -1, 1, 2)]
    barrier = pltpu.get_barrier_semaphore()
    for peer in peers:
        pl.semaphore_signal(barrier, inc=1, device_id=peer, device_id_type=MESH)

    rows = lax.broadcasted_iota(jnp.int32, (C, C), 0)
    cols = lax.broadcasted_iota(jnp.int32, (C, C), 1)
    causal, anti = rows >= cols, rows <= cols
    small[0].wait()
    small[1].wait()
    beta_row = 1.0 / (1.0 + jnp.exp(-bl[...]))
    beta = jnp.sum(jnp.where(rows == cols, beta_row, 0.0), axis=1, keepdims=True)
    cum = jnp.sum(jnp.where(cols <= rows, ld[...], 0.0), axis=1, keepdims=True)
    cum_row = jnp.sum(jnp.where(rows == cols, cum, 0.0), axis=0, keepdims=True)
    total = cum[C - 1 : C, :]
    decay = jnp.exp(-jnp.abs(cum - cum_row))
    opening = jnp.exp(cum)
    fading = jnp.exp(total - cum)

    def weights(at_rows):
        return jnp.concatenate([wgt[p, at_rows, :] for p in range(3)], axis=1)

    proj = None
    for k in range(K_PARTS):
        for copy in parts[k]:
            copy.wait()
        rows_k = pl.ds(k * K_PART, K_PART)
        term = jnp.dot(tok[:, rows_k], weights(rows_k), preferred_element_type=F32)
        proj = term if proj is None else proj + term
    small[2].wait()
    q, key, v = proj[:, :DK], proj[:, DK : 2 * DK], proj[:, 2 * DK :]
    q_inv = lax.rsqrt(jnp.sum(q * q, axis=1, keepdims=True) + 1e-6)
    k_inv = lax.rsqrt(jnp.sum(key * key, axis=1, keepdims=True) + 1e-6)
    qn, kn = q * q_inv, key * k_inv
    g = og[...]

    kb = kn.astype(BF16)
    qb = qn.astype(BF16)
    low = beta * jnp.where(rows > cols, decay * dot(kb, kb, 1, 1), 0.0)
    off = unit_inverse_less_identity(low, rows, cols).astype(BF16)
    bk = opening * kn
    fk = fading * kn
    x0 = beta * bk
    xs = x0 + dot(off, x0)
    xf = beta * (fk + dot(off, fk, 0, 0))
    r_seg = -dot(xf, bk, 0, 0)
    a_seg = jnp.broadcast_to(jnp.exp(total), (1, DK))

    def put_r(ref, a, r):
        ref[pl.ds(R_AT, DK), :] = r.astype(BF16)
        place = lax.broadcasted_iota(jnp.int32, (16, DK), 0)
        first, second, third = [t.astype(F32) for t in thirds(a)]
        tile = jnp.where(place == 0, first, jnp.where(place == 1, second, jnp.where(place == 2, third, 0.0)))
        ref[pl.ds(A_AT, 16), :] = tile.astype(BF16)

    def put(ref, a, r, b, zz):
        put_r(ref, a, r)
        ref[pl.ds(B_AT, DK), :] = b.astype(BF16)
        ref[pl.ds(Z_AT, DK), :] = zz.astype(BF16)

    def scale_of(ref):
        return jnp.sum(ref[pl.ds(A_AT, 16), :].astype(F32), axis=0, keepdims=True)

    def pair_copy(piece, slot):
        start, size = PIECES[piece]
        part = ag.at[slot, pl.ds(start, size)]
        return pltpu.make_async_remote_copy(
            src_ref=part, dst_ref=part, send_sem=a_s.at[piece], recv_sem=a_r.at[piece],
            device_id=at(dy=-way), device_id_type=MESH,
        )

    put_r(ag.at[odd], a_seg, r_seg)
    pl.semaphore_wait(barrier, len(peers))
    pair_copy(0, odd).start()
    v0 = beta * v
    w0 = v0 + dot(off, v0)
    fk_hi, fk_lo = split(fk)
    w_hi, w_lo = split(w0)
    b_seg = dot(fk_hi, w_hi, 0, 0) + (dot(fk_lo, w_hi, 0, 0) + dot(fk_hi, w_lo, 0, 0))
    ag[odd, pl.ds(B_AT, DK), :] = b_seg.astype(BF16)
    pair_copy(1, odd).start()
    pg = dot(jnp.where(anti, decay * dot(kb, qb, 1, 1), 0.0), g)
    z_seg = dot(opening * qn, g, 0, 0) - dot(xs, pg, 0, 0)
    ag[odd, pl.ds(Z_AT, DK), :] = z_seg.astype(BF16)
    pair_copy(2, odd).start()
    y0 = beta * (pg + dot(off, pg, 0, 0))

    def leaf(ref):
        r = ref[pl.ds(R_AT, DK), :].astype(F32)
        return (
            scale_of(ref), r, r.T, ref[pl.ds(B_AT, DK), :].astype(F32), ref[pl.ds(Z_AT, DK), :].astype(F32)
        )

    def wide(left, right):
        return jnp.concatenate([left, right], axis=1)

    def ahead(early, late):
        a0, r0, _, b0, _ = early
        a1, r1, _, b1, _ = late
        both = dot(r1, wide(r0, b0))
        return a0 * a1, a1 * r0 + a0 * r1 + both[:, :DK], a1 * b0 + b1 + both[:, DK:]

    def behind(early, late):
        a0, _, t0, _, z0 = early
        a1, _, t1, _, z1 = late
        both = dot(t0, wide(t1, z1))
        return a0 * a1, a1 * t0 + a0 * t1 + both[:, :DK], a0 * z1 + z0 + both[:, DK:]

    def compose(early, late):
        a, r, b = ahead(early, late)
        _, t, zz = behind(early, late)
        return a, r, t, b, zz

    def pick(flag, one, other):
        return tuple(jnp.where(flag, p, o) for p, o in zip(one, other))

    for piece in range(3):
        pair_copy(piece, 1 - odd).wait_recv()
    early, late = leaf(ag.at[0]), leaf(ag.at[1])
    a_pair, r_pair, b_pair = ahead(early, late)
    _, _, z_pair = behind(early, late)

    put(qg.at[pair], a_pair, r_pair, b_pair, z_pair)

    def row_copy(m, slot):
        part = qg.at[slot]
        return pltpu.make_async_remote_copy(
            src_ref=part, dst_ref=part, send_sem=q_s.at[m], recv_sem=q_r.at[m],
            device_id=at(dy=m * way), device_id_type=MESH,
        )

    for m in (3, 2, 1):
        row_copy(m, pair).start()
    for m, shift in ((1, way), (2, -way), (3, 2)):
        row_copy(m, (pair + shift + 4) % 4).wait_recv()
    pairs = [leaf(qg.at[j]) for j in range(4)]
    quads = [compose(pairs[0], pairs[1]), compose(pairs[2], pairs[3])]
    a_row, r_row, b_row = ahead(quads[0], quads[1])
    _, _, z_row = behind(quads[0], quads[1])

    put(xg.at[x], a_row, r_row, b_row, z_row)
    x_copies = []
    for m in (2, 1, 3):
        start = pl.multiple_of(jnp.where(x + m < X, B_AT, R_AT), 128)
        part = xg.at[x, pl.ds(start, 272)]
        x_copies.append(
            pltpu.make_async_remote_copy(
                src_ref=part, dst_ref=part, send_sem=x_s.at[m], recv_sem=x_r.at[m],
                device_id=at(dx=m), device_id_type=MESH,
            )
        )
        x_copies[-1].start()

    zero = jnp.zeros((DK, DK), F32)
    none = (jnp.ones((1, DK), F32), zero, zero, zero, zero)
    four, two, one = y >= 4, y % 4 >= 2, y % 2 == 1
    before = pick(four, quads[0], none)
    second = pick(two, pick(four, pairs[2], pairs[0]), none)
    third = pick(one, early, none)
    a_pre, r_pre, b_pre = ahead(before, second)
    a_pre, r_pre, b_pre = ahead((a_pre, r_pre, None, b_pre, None), third)
    first = pick(one, none, late)
    second = pick(two, none, pick(four, pairs[3], pairs[1]))
    last = pick(four, none, quads[1])
    a_suf, t_suf, z_suf = behind(second, last)
    a_suf, t_suf, z_suf = behind(first, (a_suf, None, t_suf, None, z_suf))

    for m in (1, 3, 2):
        source = (x - m + X) % X
        start = pl.multiple_of(jnp.where(source < x, B_AT, R_AT), 128)
        part = xg.at[source, pl.ds(start, 272)]
        pltpu.make_async_remote_copy(
            src_ref=part, dst_ref=part, send_sem=x_s.at[m], recv_sem=x_r.at[m],
            device_id=at(dx=m), device_id_type=MESH,
        ).wait_recv()
    state, seed = zero, zero
    for j in range(X - 1):
        i = X - 1 - j
        r_j, r_i = xg[j, pl.ds(R_AT, DK), :], xg[i, pl.ds(R_AT, DK), :]
        grown = xg[j, pl.ds(B_AT, DK), :].astype(F32)
        if j:
            grown = grown + scale_of(xg.at[j]) * state + dot(r_j, state)
        state = jnp.where(j < x, grown, state)
        grown = xg[i, pl.ds(Z_AT, DK), :].astype(F32)
        if j:
            grown = grown + scale_of(xg.at[i]) * seed + dot(r_i, seed, 0, 0)
        seed = jnp.where(i > x, grown, seed)
    s_in = a_pre * state + dot(r_pre, state) + b_pre
    g_out = a_suf * seed + dot(t_suf, seed) + z_suf

    w = w0 - dot(xs, s_in)
    yy = y0 + dot(xf, g_out)
    wb, yb = w.astype(BF16), yy.astype(BF16)
    s_hi, s_lo = split(s_in)
    e = jnp.where(causal, decay * dot(g, wb, 1, 1), 0.0)
    et = jnp.where(anti, decay * dot(wb, g, 1, 1), 0.0)
    h = jnp.where(rows > cols, dot(yb, wb, 1, 1), dot(wb, yb, 1, 1)) * decay
    h = jnp.where(rows == cols, 0.0, h)
    dq = opening * (dot(g, s_hi, 1, 1) + dot(g, s_lo, 1, 1)) + dot(e, kb)
    dk = fading * dot(wb, g_out, 1, 1) + dot(et, qb) - dot(h, kb) - opening * dot(yb, s_hi, 1, 1)
    dq = q_inv * (dq - qn * jnp.sum(qn * dq, axis=1, keepdims=True))
    dk = k_inv * (dk - kn * jnp.sum(kn * dk, axis=1, keepdims=True))
    grads = jnp.concatenate([dq, dk, yy], axis=1).astype(BF16)

    def core_copy(turn):
        return pltpu.make_async_remote_copy(
            src_ref=core_out.at[turn], dst_ref=core_in.at[turn], send_sem=c_s.at[turn],
            recv_sem=c_r.at[turn], device_id=at(dc=1), device_id_type=MESH,
        )

    def z_copy(hop):
        turn, start, size, to = HOPS[hop]
        part = pl.ds(start, size)
        return pltpu.make_async_remote_copy(
            src_ref=z_out.at[turn, part], dst_ref=z_in.at[turn, part], send_sem=z_s.at[hop],
            recv_sem=z_r.at[hop], device_id=at(dz=to), device_id_type=MESH,
        )

    def product(turn):
        to = pl.multiple_of(((z + ORDER[turn] + Z) % Z) * 2 * DK, 2 * DK)
        weight = weights(pl.ds(to, 2 * DK))
        both = dot(grads, weight, 1, 1)
        left, right = both[:, :DK], both[:, DK:]
        core_out[turn] = jnp.where(core == 0, right, left).astype(BF16)
        core_copy(turn).start()
        own[turn] = jnp.where(core == 0, left, right)

    def pass_on(turn):
        core_copy(turn).wait_recv()
        mine = own[turn] + core_in[turn].astype(F32)
        if turn == 5:
            z_copy(0).wait_recv()
            z_copy(2).wait_recv()
            far = jnp.concatenate([z_in[0, :128, :].astype(F32), jnp.zeros((128, DK), F32)], axis=0)
            mine = mine + far + z_in[1].astype(F32)
        elif turn == 6:
            z_copy(1).wait_recv()
            z_copy(3).wait_recv()
            far = jnp.concatenate([jnp.zeros((128, DK), F32), z_in[0, 128:, :].astype(F32)], axis=0)
            mine = mine + far + z_in[2].astype(F32)
        z_out[turn] = mine.astype(BF16)
        for hop in (0, 1) if turn == 0 else (turn + 1,):
            z_copy(hop).start()

    for turn in range(Z):
        product(turn)
        if turn >= LAG:
            pass_on(turn - LAG)
    for turn in range(Z - LAG, Z - 1):
        pass_on(turn)
    core_copy(Z - 1).wait_recv()
    mine = own[Z - 1] + core_in[Z - 1].astype(F32)
    for turn in range(3, Z - 1):
        z_copy(turn + 1).wait_recv()
        mine = mine + z_in[turn].astype(F32)
    out[...] = mine.astype(BF16)

    for piece in range(3):
        pair_copy(piece, odd).wait_send()
    for m in (1, 2, 3):
        row_copy(m, pair).wait_send()
    for copy in x_copies:
        copy.wait_send()
    for turn in range(Z):
        core_copy(turn).wait_send()
        z_copy(turn).wait_send()


def on_device(tokens, qkv_weight, beta_logit, log_decay, out_grad):
    dma = pltpu.SemaphoreType.DMA
    return pl.pallas_call(
        kernel,
        out_shape=jax.ShapeDtypeStruct((C, DK), BF16),
        in_specs=[pl.BlockSpec(memory_space=pl.ANY)] * 5,
        out_specs=pl.BlockSpec(memory_space=pltpu.VMEM),
        scratch_shapes=[
            pltpu.VMEM((C, K_PARTS * K_PART), BF16),
            pltpu.VMEM((3, K_PARTS * K_PART, DK), BF16),
            pltpu.VMEM((1, C), F32),
            pltpu.VMEM((1, C), F32),
            pltpu.VMEM((C, DK), BF16),
            pltpu.VMEM((2, ROWS, DK), BF16),
            pltpu.VMEM((4, ROWS, DK), BF16),
            pltpu.VMEM((X, ROWS, DK), BF16),
            pltpu.VMEM((Z, C, DK), BF16),
            pltpu.VMEM((Z, C, DK), BF16),
            pltpu.VMEM((Z, C, DK), F32),
            pltpu.VMEM((Z - 1, C, DK), BF16),
            pltpu.VMEM((Z - 1, C, DK), BF16),
            dma((3 + K_PARTS,)), dma((K_PARTS, 3)),
            dma((3,)), dma((3,)), dma((4,)), dma((4,)), dma((X,)), dma((X,)),
            dma((Z,)), dma((Z,)), dma((Z,)), dma((Z,)),
        ],
        compiler_params=pltpu.CompilerParams(
            collective_id=0, has_side_effects=True, vmem_limit_bytes=63 * 2**20
        ),
        name="delta_rule",
    )(tokens, qkv_weight, beta_logit, log_decay, out_grad)


def solution(mesh):
    return jax.shard_map(
        on_device,
        mesh=mesh,
        in_specs=(
            P("seq", None),
            P(None, None, "head"),
            P("head", "seq"),
            P("head", "seq"),
            P("seq", "head"),
        ),
        out_specs=P("seq", "head"),
        check_vma=False,
    )
```

```python
import functools

import jax
import jax.numpy as jnp
from jax import lax
from jax.experimental import pallas as pl
from jax.experimental.pallas import tpu as pltpu
from jax.sharding import PartitionSpec as P

F32 = jnp.float32
BF16 = jnp.bfloat16
MESH = pl.DeviceIdType.MESH
X, Y, Z = 4, 8, 8
C, DK = 256, 128
B_AT, R_AT, A_AT, Z_AT, ROWS = 0, 128, 256, 272, 400
PIECES = ((R_AT, 144), (B_AT, 128), (Z_AT, 128))
K_PARTS, K_PART = 2, 1024
ORDER = (4, 3, -3, 1, -1, 2, -2, 0)
HOPS = (
    (0, 0, 128, 2), (0, 128, 128, -2),
    (1, 0, 128, 1), (1, 128, 128, 1), (2, 0, 128, -1), (2, 128, 128, -1),
    (3, 0, 256, 1), (4, 0, 256, -1),
    (5, 0, 128, 2), (5, 128, 128, 2), (6, 0, 128, -2), (6, 128, 128, -2),
)
SENDS = ((0, 1), (3, 2), (4, 5), (6,), (7,))
ADDS = ((9, (3,)), (10, (4,)), (8, (0, 2)), (11, (1, 5)))
LAG = 3


def dot(a, b, ca=1, cb=0):
    return lax.dot_general(
        a.astype(BF16), b.astype(BF16), (((ca,), (cb,)), ((), ())), preferred_element_type=F32
    )


def split(a):
    upper = a.astype(BF16)
    return upper, (a - upper.astype(F32)).astype(BF16)


def thirds(a):
    upper, rest = split(a)
    middle = rest
    lower = (a - upper.astype(F32) - middle.astype(F32)).astype(BF16)
    return upper, middle, lower


def unit_inverse_less_identity(low, rows, cols):
    def same(shift):
        return (rows >> shift) == (cols >> shift)

    power = jnp.where(same(5), low, 0.0)
    off = -power
    for _ in range(4):
        power = dot(power, power)
        off = off + power + dot(off, power)
    for shift in (5, 6, 7):
        inside = jnp.where(same(shift + 1) & ~same(shift), low, 0.0)
        left = inside + dot(off, inside)
        off = off - left - dot(left, off)
    return off


def kernel(
    tok_hbm, wgt_hbm, bl_hbm, ld_hbm, og_hbm, out,
    tok, wgt, bl, ld, og, ag, qg, xg, core_out, core_in, own, z_out, z_in,
    in_sem, w_sem, a_s, a_r, q_s, q_r, x_s, x_r, c_s, c_r, z_s, z_r,
):
    seq, head = lax.axis_index("seq"), lax.axis_index("head")
    x, y = seq // Y, seq % Y
    z, core = head // 2, head % 2

    def at(dx=0, dy=0, dz=0, dc=0):
        return (
            ((x + dx) % X) * Y + (y + dy + Y) % Y,
            ((z + dz + Z) % Z) * 2 + (core + dc) % 2,
        )

    small = [
        pltpu.make_async_copy(src, dst, in_sem.at[i])
        for i, (src, dst) in enumerate(((ld_hbm, ld), (bl_hbm, bl), (og_hbm, og)))
    ]
    parts = []
    for k in range(K_PARTS):
        rows_k = pl.ds(k * K_PART, K_PART)
        parts.append(
            [pltpu.make_async_copy(tok_hbm.at[:, rows_k], tok.at[:, rows_k], in_sem.at[3 + k])]
            + [
                pltpu.make_async_copy(
                    wgt_hbm.at[p, rows_k, :], wgt.at[p, rows_k, :], w_sem.at[k, p]
                )
                for p in range(3)
            ]
        )
    for copy in small[:2] + sum(parts, []) + small[2:]:
        copy.start()
    pair, odd = y // 2, y % 2
    way = 2 * odd - 1
    peers = [at(dy=m * way) for m in (-2, -1, 1, 2, 3)]
    peers += [at(dx=m) for m in (1, 2, 3)] + [at(dc=1)] + [at(dz=m) for m in (-2, -1, 1, 2)]
    barrier = pltpu.get_barrier_semaphore()
    for peer in peers:
        pl.semaphore_signal(barrier, inc=1, device_id=peer, device_id_type=MESH)

    rows = lax.broadcasted_iota(jnp.int32, (C, C), 0)
    cols = lax.broadcasted_iota(jnp.int32, (C, C), 1)
    causal, anti = rows >= cols, rows <= cols
    small[0].wait()
    small[1].wait()
    beta_row = 1.0 / (1.0 + jnp.exp(-bl[...]))
    beta = jnp.sum(jnp.where(rows == cols, beta_row, 0.0), axis=1, keepdims=True)
    cum = jnp.sum(jnp.where(cols <= rows, ld[...], 0.0), axis=1, keepdims=True)
    cum_row = jnp.sum(jnp.where(rows == cols, cum, 0.0), axis=0, keepdims=True)
    total = cum[C - 1 : C, :]
    decay = jnp.exp(-jnp.abs(cum - cum_row))
    opening = jnp.exp(cum)
    fading = jnp.exp(total - cum)

    def weights(at_rows):
        return jnp.concatenate([wgt[p, at_rows, :] for p in range(3)], axis=1)

    proj = None
    for k in range(K_PARTS):
        for copy in parts[k]:
            copy.wait()
        rows_k = pl.ds(k * K_PART, K_PART)
        term = jnp.dot(tok[:, rows_k], weights(rows_k), preferred_element_type=F32)
        proj = term if proj is None else proj + term
    small[2].wait()
    q, key, v = proj[:, :DK], proj[:, DK : 2 * DK], proj[:, 2 * DK :]
    q_inv = lax.rsqrt(jnp.sum(q * q, axis=1, keepdims=True) + 1e-6)
    k_inv = lax.rsqrt(jnp.sum(key * key, axis=1, keepdims=True) + 1e-6)
    qn, kn = q * q_inv, key * k_inv
    g = og[...]

    kb = kn.astype(BF16)
    qb = qn.astype(BF16)
    low = beta * jnp.where(rows > cols, decay * dot(kb, kb, 1, 1), 0.0)
    off = unit_inverse_less_identity(low, rows, cols).astype(BF16)
    bk = opening * kn
    fk = fading * kn
    x0 = beta * bk
    xs = x0 + dot(off, x0)
    xf = beta * (fk + dot(off, fk, 0, 0))
    r_seg = -dot(xf, bk, 0, 0)
    a_seg = jnp.broadcast_to(jnp.exp(total), (1, DK))

    def put_r(ref, a, r):
        ref[pl.ds(R_AT, DK), :] = r.astype(BF16)
        place = lax.broadcasted_iota(jnp.int32, (16, DK), 0)
        first, second, third = [t.astype(F32) for t in thirds(a)]
        tile = jnp.where(place == 0, first, jnp.where(place == 1, second, jnp.where(place == 2, third, 0.0)))
        ref[pl.ds(A_AT, 16), :] = tile.astype(BF16)

    def put(ref, a, r, b, zz):
        put_r(ref, a, r)
        ref[pl.ds(B_AT, DK), :] = b.astype(BF16)
        ref[pl.ds(Z_AT, DK), :] = zz.astype(BF16)

    def scale_of(ref):
        return jnp.sum(ref[pl.ds(A_AT, 16), :].astype(F32), axis=0, keepdims=True)

    def pair_copy(piece, slot):
        start, size = PIECES[piece]
        part = ag.at[slot, pl.ds(start, size)]
        return pltpu.make_async_remote_copy(
            src_ref=part, dst_ref=part, send_sem=a_s.at[piece], recv_sem=a_r.at[piece],
            device_id=at(dy=-way), device_id_type=MESH,
        )

    put_r(ag.at[odd], a_seg, r_seg)
    pl.semaphore_wait(barrier, len(peers))
    pair_copy(0, odd).start()
    v0 = beta * v
    w0 = v0 + dot(off, v0)
    fk_hi, fk_lo = split(fk)
    w_hi, w_lo = split(w0)
    b_seg = dot(fk_hi, w_hi, 0, 0) + (dot(fk_lo, w_hi, 0, 0) + dot(fk_hi, w_lo, 0, 0))
    ag[odd, pl.ds(B_AT, DK), :] = b_seg.astype(BF16)
    pair_copy(1, odd).start()
    pg = dot(jnp.where(anti, decay * dot(kb, qb, 1, 1), 0.0), g)
    z_seg = dot(opening * qn, g, 0, 0) - dot(xs, pg, 0, 0)
    ag[odd, pl.ds(Z_AT, DK), :] = z_seg.astype(BF16)
    pair_copy(2, odd).start()
    y0 = beta * (pg + dot(off, pg, 0, 0))

    def leaf(ref):
        r = ref[pl.ds(R_AT, DK), :].astype(F32)
        return (
            scale_of(ref), r, r.T, ref[pl.ds(B_AT, DK), :].astype(F32), ref[pl.ds(Z_AT, DK), :].astype(F32)
        )

    def wide(left, right):
        return jnp.concatenate([left, right], axis=1)

    def ahead(early, late):
        a0, r0, _, b0, _ = early
        a1, r1, _, b1, _ = late
        both = dot(r1, wide(r0, b0))
        return a0 * a1, a1 * r0 + a0 * r1 + both[:, :DK], a1 * b0 + b1 + both[:, DK:]

    def behind(early, late):
        a0, _, t0, _, z0 = early
        a1, _, t1, _, z1 = late
        both = dot(t0, wide(t1, z1))
        return a0 * a1, a1 * t0 + a0 * t1 + both[:, :DK], a0 * z1 + z0 + both[:, DK:]

    def compose(early, late):
        a, r, b = ahead(early, late)
        _, t, zz = behind(early, late)
        return a, r, t, b, zz

    def pick(flag, one, other):
        return tuple(jnp.where(flag, p, o) for p, o in zip(one, other))

    for piece in range(3):
        pair_copy(piece, 1 - odd).wait_recv()
    early, late = leaf(ag.at[0]), leaf(ag.at[1])
    a_pair, r_pair, b_pair = ahead(early, late)
    _, _, z_pair = behind(early, late)

    put(qg.at[pair], a_pair, r_pair, b_pair, z_pair)

    def row_copy(m, slot):
        part = qg.at[slot]
        return pltpu.make_async_remote_copy(
            src_ref=part, dst_ref=part, send_sem=q_s.at[m], recv_sem=q_r.at[m],
            device_id=at(dy=m * way), device_id_type=MESH,
        )

    for m in (3, 2, 1):
        row_copy(m, pair).start()
    for m, shift in ((1, way), (2, -way), (3, 2)):
        row_copy(m, (pair + shift + 4) % 4).wait_recv()
    pairs = [leaf(qg.at[j]) for j in range(4)]
    quads = [compose(pairs[0], pairs[1]), compose(pairs[2], pairs[3])]
    a_row, r_row, b_row = ahead(quads[0], quads[1])
    _, _, z_row = behind(quads[0], quads[1])

    put(xg.at[x], a_row, r_row, b_row, z_row)
    x_copies = []
    for m in (2, 1, 3):
        start = pl.multiple_of(jnp.where(x + m < X, B_AT, R_AT), 128)
        part = xg.at[x, pl.ds(start, 272)]
        x_copies.append(
            pltpu.make_async_remote_copy(
                src_ref=part, dst_ref=part, send_sem=x_s.at[m], recv_sem=x_r.at[m],
                device_id=at(dx=m), device_id_type=MESH,
            )
        )
        x_copies[-1].start()

    zero = jnp.zeros((DK, DK), F32)
    none = (jnp.ones((1, DK), F32), zero, zero, zero, zero)
    four, two, one = y >= 4, y % 4 >= 2, y % 2 == 1
    before = pick(four, quads[0], none)
    second = pick(two, pick(four, pairs[2], pairs[0]), none)
    third = pick(one, early, none)
    a_pre, r_pre, b_pre = ahead(before, second)
    a_pre, r_pre, b_pre = ahead((a_pre, r_pre, None, b_pre, None), third)
    first = pick(one, none, late)
    second = pick(two, none, pick(four, pairs[3], pairs[1]))
    last = pick(four, none, quads[1])
    a_suf, t_suf, z_suf = behind(second, last)
    a_suf, t_suf, z_suf = behind(first, (a_suf, None, t_suf, None, z_suf))

    for m in (1, 3, 2):
        source = (x - m + X) % X
        start = pl.multiple_of(jnp.where(source < x, B_AT, R_AT), 128)
        part = xg.at[source, pl.ds(start, 272)]
        pltpu.make_async_remote_copy(
            src_ref=part, dst_ref=part, send_sem=x_s.at[m], recv_sem=x_r.at[m],
            device_id=at(dx=m), device_id_type=MESH,
        ).wait_recv()
    state, seed = zero, zero
    for j in range(X - 1):
        i = X - 1 - j
        r_j, r_i = xg[j, pl.ds(R_AT, DK), :], xg[i, pl.ds(R_AT, DK), :]
        grown = xg[j, pl.ds(B_AT, DK), :].astype(F32)
        if j:
            grown = grown + scale_of(xg.at[j]) * state + dot(r_j, state)
        state = jnp.where(j < x, grown, state)
        grown = xg[i, pl.ds(Z_AT, DK), :].astype(F32)
        if j:
            grown = grown + scale_of(xg.at[i]) * seed + dot(r_i, seed, 0, 0)
        seed = jnp.where(i > x, grown, seed)
    s_in = a_pre * state + dot(r_pre, state) + b_pre
    g_out = a_suf * seed + dot(t_suf, seed) + z_suf

    w = w0 - dot(xs, s_in)
    yy = y0 + dot(xf, g_out)
    wb, yb = w.astype(BF16), yy.astype(BF16)
    s_hi, s_lo = split(s_in)
    e = jnp.where(causal, decay * dot(g, wb, 1, 1), 0.0)
    et = jnp.where(anti, decay * dot(wb, g, 1, 1), 0.0)
    h = jnp.where(rows > cols, dot(yb, wb, 1, 1), dot(wb, yb, 1, 1)) * decay
    h = jnp.where(rows == cols, 0.0, h)
    dq = opening * (dot(g, s_hi, 1, 1) + dot(g, s_lo, 1, 1)) + dot(e, kb)
    dk = fading * dot(wb, g_out, 1, 1) + dot(et, qb) - dot(h, kb) - opening * dot(yb, s_hi, 1, 1)
    dq = q_inv * (dq - qn * jnp.sum(qn * dq, axis=1, keepdims=True))
    dk = k_inv * (dk - kn * jnp.sum(kn * dk, axis=1, keepdims=True))
    grads = jnp.concatenate([dq, dk, yy], axis=1).astype(BF16)

    def core_copy(turn):
        return pltpu.make_async_remote_copy(
            src_ref=core_out.at[turn], dst_ref=core_in.at[turn], send_sem=c_s.at[turn],
            recv_sem=c_r.at[turn], device_id=at(dc=1), device_id_type=MESH,
        )

    def z_copy(hop):
        turn, start, size, to = HOPS[hop]
        part = pl.ds(start, size)
        return pltpu.make_async_remote_copy(
            src_ref=z_out.at[turn, part], dst_ref=z_in.at[turn, part], send_sem=z_s.at[hop],
            recv_sem=z_r.at[hop], device_id=at(dz=to), device_id_type=MESH,
        )

    def product(turn):
        to = pl.multiple_of(((z + ORDER[turn] + Z) % Z) * 2 * DK, 2 * DK)
        weight = weights(pl.ds(to, 2 * DK))
        both = dot(grads, weight, 1, 1)
        left, right = both[:, :DK], both[:, DK:]
        core_out[turn] = jnp.where(core == 0, right, left).astype(BF16)
        core_copy(turn).start()
        own[turn] = jnp.where(core == 0, left, right)

    def pass_on(turn):
        core_copy(turn).wait_recv()
        z_out[turn] = (own[turn] + core_in[turn].astype(F32)).astype(BF16)
        for hop in SENDS[turn]:
            z_copy(hop).start()

    for turn in range(Z):
        product(turn)
        if LAG <= turn < LAG + 5:
            pass_on(turn - LAG)
    core_copy(5).wait_recv()
    core_copy(6).wait_recv()
    for hop, joins in ADDS:
        turn, start, size, _ = HOPS[hop]
        part = pl.ds(start, size)
        mine = own[turn, part, :] + core_in[turn, part, :].astype(F32)
        for other in joins:
            z_copy(other).wait_recv()
            mine = mine + z_in[HOPS[other][0], part, :].astype(F32)
        z_out[turn, part, :] = mine.astype(BF16)
        z_copy(hop).start()
    core_copy(Z - 1).wait_recv()
    z_copy(6).wait_recv()
    z_copy(7).wait_recv()
    mine = own[Z - 1] + core_in[Z - 1].astype(F32) + z_in[3].astype(F32) + z_in[4].astype(F32)
    for hop in (9, 10, 8, 11):
        z_copy(hop).wait_recv()
    mine = mine + z_in[5].astype(F32) + z_in[6].astype(F32)
    out[...] = mine.astype(BF16)

    for piece in range(3):
        pair_copy(piece, odd).wait_send()
    for m in (1, 2, 3):
        row_copy(m, pair).wait_send()
    for copy in x_copies:
        copy.wait_send()
    for turn in range(Z):
        core_copy(turn).wait_send()
    for hop in range(len(HOPS)):
        z_copy(hop).wait_send()


def on_device(tokens, qkv_weight, beta_logit, log_decay, out_grad):
    dma = pltpu.SemaphoreType.DMA
    return pl.pallas_call(
        kernel,
        out_shape=jax.ShapeDtypeStruct((C, DK), BF16),
        in_specs=[pl.BlockSpec(memory_space=pl.ANY)] * 5,
        out_specs=pl.BlockSpec(memory_space=pltpu.VMEM),
        scratch_shapes=[
            pltpu.VMEM((C, K_PARTS * K_PART), BF16),
            pltpu.VMEM((3, K_PARTS * K_PART, DK), BF16),
            pltpu.VMEM((1, C), F32),
            pltpu.VMEM((1, C), F32),
            pltpu.VMEM((C, DK), BF16),
            pltpu.VMEM((2, ROWS, DK), BF16),
            pltpu.VMEM((4, ROWS, DK), BF16),
            pltpu.VMEM((X, ROWS, DK), BF16),
            pltpu.VMEM((Z, C, DK), BF16),
            pltpu.VMEM((Z, C, DK), BF16),
            pltpu.VMEM((Z, C, DK), F32),
            pltpu.VMEM((Z - 1, C, DK), BF16),
            pltpu.VMEM((Z - 1, C, DK), BF16),
            dma((3 + K_PARTS,)), dma((K_PARTS, 3)),
            dma((3,)), dma((3,)), dma((4,)), dma((4,)), dma((X,)), dma((X,)),
            dma((Z,)), dma((Z,)), dma((len(HOPS),)), dma((len(HOPS),)),
        ],
        compiler_params=pltpu.CompilerParams(
            collective_id=0, has_side_effects=True, vmem_limit_bytes=63 * 2**20
        ),
        name="delta_rule",
    )(tokens, qkv_weight, beta_logit, log_decay, out_grad)


def solution(mesh):
    return jax.shard_map(
        on_device,
        mesh=mesh,
        in_specs=(
            P("seq", None),
            P(None, None, "head"),
            P("head", "seq"),
            P("head", "seq"),
            P("seq", "head"),
        ),
        out_specs=P("seq", "head"),
        check_vma=False,
    )
```

```python
import functools

import jax
import jax.numpy as jnp
from jax import lax
from jax.experimental import pallas as pl
from jax.experimental.pallas import tpu as pltpu
from jax.sharding import PartitionSpec as P

F32 = jnp.float32
BF16 = jnp.bfloat16
MESH = pl.DeviceIdType.MESH
X, Y, Z = 4, 8, 8
C, DK = 256, 128
B_AT, R_AT, A_AT, Z_AT, ROWS = 0, 128, 256, 272, 400
PIECES = ((R_AT, 144), (B_AT, 128), (Z_AT, 128))
K_PARTS, K_PART = 2, 1024
ORDER = (4, 3, -3, 1, -1, 2, -2, 0)
HOPS = (
    (0, 0, 128, 2), (0, 128, 128, -2),
    (1, 0, 128, 1), (1, 128, 128, 1), (2, 0, 128, -1), (2, 128, 128, -1),
    (3, 0, 256, 1), (4, 0, 256, -1),
    (5, 0, 128, 2), (5, 128, 128, 2), (6, 0, 128, -2), (6, 128, 128, -2),
)
SENDS = ((0, 1), (3, 2), (4, 5), (6,), (7,))
ADDS = ((9, (3,)), (10, (4,)), (8, (0, 2)), (11, (1, 5)))
LAG = 3


def dot(a, b, ca=1, cb=0):
    return lax.dot_general(
        a.astype(BF16), b.astype(BF16), (((ca,), (cb,)), ((), ())), preferred_element_type=F32
    )


def split(a):
    upper = a.astype(BF16)
    return upper, (a - upper.astype(F32)).astype(BF16)


def thirds(a):
    upper, rest = split(a)
    middle = rest
    lower = (a - upper.astype(F32) - middle.astype(F32)).astype(BF16)
    return upper, middle, lower


def unit_inverse_less_identity(low, rows, cols):
    def same(shift):
        return (rows >> shift) == (cols >> shift)

    power = jnp.where(same(5), low, 0.0)
    off = -power
    for _ in range(4):
        power = dot(power, power)
        off = off + power + dot(off, power)
    for shift in (5, 6, 7):
        inside = jnp.where(same(shift + 1) & ~same(shift), low, 0.0)
        left = inside + dot(off, inside)
        off = off - left - dot(left, off)
    return off


def kernel(
    tok_hbm, wgt_hbm, bl_hbm, ld_hbm, og_hbm, out,
    tok, wgt, bl, ld, og, ag, qg, xg, core_out, core_in, own, z_out, z_in,
    in_sem, w_sem, a_s, a_r, q_s, q_r, x_s, x_r, c_s, c_r, z_s, z_r,
):
    seq, head = lax.axis_index("seq"), lax.axis_index("head")
    x, y = seq // Y, seq % Y
    z, core = head // 2, head % 2

    def at(dx=0, dy=0, dz=0, dc=0):
        return (
            ((x + dx) % X) * Y + (y + dy + Y) % Y,
            ((z + dz + Z) % Z) * 2 + (core + dc) % 2,
        )

    small = [
        pltpu.make_async_copy(src, dst, in_sem.at[i])
        for i, (src, dst) in enumerate(((ld_hbm, ld), (bl_hbm, bl), (og_hbm, og)))
    ]
    parts = []
    for k in range(K_PARTS):
        rows_k = pl.ds(k * K_PART, K_PART)
        parts.append(
            [pltpu.make_async_copy(tok_hbm.at[:, rows_k], tok.at[:, rows_k], in_sem.at[3 + k])]
            + [
                pltpu.make_async_copy(
                    wgt_hbm.at[p, rows_k, :], wgt.at[p, rows_k, :], w_sem.at[k, p]
                )
                for p in range(3)
            ]
        )
    for copy in small[:2] + sum(parts, []) + small[2:]:
        copy.start()
    pair, odd = y // 2, y % 2
    way = 2 * odd - 1
    peers = [at(dy=m * way) for m in (-2, -1, 1, 2)]
    peers += [at(dx=m) for m in (1, 2, 3)] + [at(dc=1)] + [at(dz=m) for m in (-2, -1, 1, 2)]
    barrier = pltpu.get_barrier_semaphore()
    for peer in peers:
        pl.semaphore_signal(barrier, inc=1, device_id=peer, device_id_type=MESH)

    rows = lax.broadcasted_iota(jnp.int32, (C, C), 0)
    cols = lax.broadcasted_iota(jnp.int32, (C, C), 1)
    causal, anti = rows >= cols, rows <= cols
    small[0].wait()
    small[1].wait()
    beta_row = 1.0 / (1.0 + jnp.exp(-bl[...]))
    beta = jnp.sum(jnp.where(rows == cols, beta_row, 0.0), axis=1, keepdims=True)
    cum = jnp.sum(jnp.where(cols <= rows, ld[...], 0.0), axis=1, keepdims=True)
    cum_row = jnp.sum(jnp.where(rows == cols, cum, 0.0), axis=0, keepdims=True)
    total = cum[C - 1 : C, :]
    decay = jnp.exp(-jnp.abs(cum - cum_row))
    opening = jnp.exp(cum)
    fading = jnp.exp(total - cum)

    def weights(at_rows):
        return jnp.concatenate([wgt[p, at_rows, :] for p in range(3)], axis=1)

    proj = None
    for k in range(K_PARTS):
        for copy in parts[k]:
            copy.wait()
        rows_k = pl.ds(k * K_PART, K_PART)
        term = jnp.dot(tok[:, rows_k], weights(rows_k), preferred_element_type=F32)
        proj = term if proj is None else proj + term
    small[2].wait()
    q, key, v = proj[:, :DK], proj[:, DK : 2 * DK], proj[:, 2 * DK :]
    q_inv = lax.rsqrt(jnp.sum(q * q, axis=1, keepdims=True) + 1e-6)
    k_inv = lax.rsqrt(jnp.sum(key * key, axis=1, keepdims=True) + 1e-6)
    qn, kn = q * q_inv, key * k_inv
    g = og[...]

    kb = kn.astype(BF16)
    qb = qn.astype(BF16)
    low = beta * jnp.where(rows > cols, decay * dot(kb, kb, 1, 1), 0.0)
    off = unit_inverse_less_identity(low, rows, cols).astype(BF16)
    bk = opening * kn
    fk = fading * kn
    x0 = beta * bk
    xs = x0 + dot(off, x0)
    xf = beta * (fk + dot(off, fk, 0, 0))
    r_seg = -dot(xf, bk, 0, 0)
    a_seg = jnp.broadcast_to(jnp.exp(total), (1, DK))

    def put_r(ref, a, r):
        ref[pl.ds(R_AT, DK), :] = r.astype(BF16)
        place = lax.broadcasted_iota(jnp.int32, (16, DK), 0)
        first, second, third = [t.astype(F32) for t in thirds(a)]
        tile = jnp.where(place == 0, first, jnp.where(place == 1, second, jnp.where(place == 2, third, 0.0)))
        ref[pl.ds(A_AT, 16), :] = tile.astype(BF16)

    def put(ref, a, r, b, zz):
        put_r(ref, a, r)
        ref[pl.ds(B_AT, DK), :] = b.astype(BF16)
        ref[pl.ds(Z_AT, DK), :] = zz.astype(BF16)

    def scale_of(ref):
        return jnp.sum(ref[pl.ds(A_AT, 16), :].astype(F32), axis=0, keepdims=True)

    def pair_copy(piece, slot):
        start, size = PIECES[piece]
        part = ag.at[slot, pl.ds(start, size)]
        return pltpu.make_async_remote_copy(
            src_ref=part, dst_ref=part, send_sem=a_s.at[piece], recv_sem=a_r.at[piece],
            device_id=at(dy=-way), device_id_type=MESH,
        )

    put_r(ag.at[odd], a_seg, r_seg)
    pl.semaphore_wait(barrier, len(peers))
    pair_copy(0, odd).start()
    v0 = beta * v
    w0 = v0 + dot(off, v0)
    fk_hi, fk_lo = split(fk)
    w_hi, w_lo = split(w0)
    b_seg = dot(fk_hi, w_hi, 0, 0) + (dot(fk_lo, w_hi, 0, 0) + dot(fk_hi, w_lo, 0, 0))
    ag[odd, pl.ds(B_AT, DK), :] = b_seg.astype(BF16)
    pair_copy(1, odd).start()
    pg = dot(jnp.where(anti, decay * dot(kb, qb, 1, 1), 0.0), g)
    z_seg = dot(opening * qn, g, 0, 0) - dot(xs, pg, 0, 0)
    ag[odd, pl.ds(Z_AT, DK), :] = z_seg.astype(BF16)
    pair_copy(2, odd).start()
    y0 = beta * (pg + dot(off, pg, 0, 0))

    def leaf(ref):
        r = ref[pl.ds(R_AT, DK), :].astype(F32)
        return (
            scale_of(ref), r, r.T, ref[pl.ds(B_AT, DK), :].astype(F32), ref[pl.ds(Z_AT, DK), :].astype(F32)
        )

    def wide(left, right):
        return jnp.concatenate([left, right], axis=1)

    def ahead(early, late):
        a0, r0, _, b0, _ = early
        a1, r1, _, b1, _ = late
        both = dot(r1, wide(r0, b0))
        return a0 * a1, a1 * r0 + a0 * r1 + both[:, :DK], a1 * b0 + b1 + both[:, DK:]

    def behind(early, late):
        a0, _, t0, _, z0 = early
        a1, _, t1, _, z1 = late
        both = dot(t0, wide(t1, z1))
        return a0 * a1, a1 * t0 + a0 * t1 + both[:, :DK], a0 * z1 + z0 + both[:, DK:]

    def compose(early, late):
        a, r, b = ahead(early, late)
        _, t, zz = behind(early, late)
        return a, r, t, b, zz

    def pick(flag, one, other):
        return tuple(jnp.where(flag, p, o) for p, o in zip(one, other))

    for piece in range(3):
        pair_copy(piece, 1 - odd).wait_recv()
    early, late = leaf(ag.at[0]), leaf(ag.at[1])
    a_pair, r_pair, b_pair = ahead(early, late)
    _, _, z_pair = behind(early, late)

    put(qg.at[pair], a_pair, r_pair, b_pair, z_pair)

    def row_copy(m, piece, slot):
        start, size = PIECES[piece]
        part = qg.at[slot, pl.ds(start, size)]
        return pltpu.make_async_remote_copy(
            src_ref=part, dst_ref=part, send_sem=q_s.at[m - 1, piece], recv_sem=q_r.at[m - 1, piece],
            device_id=at(dy=(2 if m == 2 else 1) * way), device_id_type=MESH,
        )

    for m in (2, 1):
        for piece in range(3):
            row_copy(m, piece, pair).start()
    behind_us = (pair - way + 4) % 4
    for piece in range(3):
        row_copy(2, piece, behind_us).wait_recv()
        row_copy(3, piece, behind_us).start()
    for piece in range(3):
        row_copy(1, piece, (pair + way + 4) % 4).wait_recv()
    for piece in range(3):
        row_copy(3, piece, (pair + 2) % 4).wait_recv()
    pairs = [leaf(qg.at[j]) for j in range(4)]
    quads = [compose(pairs[0], pairs[1]), compose(pairs[2], pairs[3])]
    a_row, r_row, b_row = ahead(quads[0], quads[1])
    _, _, z_row = behind(quads[0], quads[1])

    put(xg.at[x], a_row, r_row, b_row, z_row)
    x_copies = []
    for m in (2, 1, 3):
        start = pl.multiple_of(jnp.where(x + m < X, B_AT, R_AT), 128)
        part = xg.at[x, pl.ds(start, 272)]
        x_copies.append(
            pltpu.make_async_remote_copy(
                src_ref=part, dst_ref=part, send_sem=x_s.at[m], recv_sem=x_r.at[m],
                device_id=at(dx=m), device_id_type=MESH,
            )
        )
        x_copies[-1].start()

    zero = jnp.zeros((DK, DK), F32)
    none = (jnp.ones((1, DK), F32), zero, zero, zero, zero)
    four, two, one = y >= 4, y % 4 >= 2, y % 2 == 1
    before = pick(four, quads[0], none)
    second = pick(two, pick(four, pairs[2], pairs[0]), none)
    third = pick(one, early, none)
    a_pre, r_pre, b_pre = ahead(before, second)
    a_pre, r_pre, b_pre = ahead((a_pre, r_pre, None, b_pre, None), third)
    first = pick(one, none, late)
    second = pick(two, none, pick(four, pairs[3], pairs[1]))
    last = pick(four, none, quads[1])
    a_suf, t_suf, z_suf = behind(second, last)
    a_suf, t_suf, z_suf = behind(first, (a_suf, None, t_suf, None, z_suf))

    for m in (1, 3, 2):
        source = (x - m + X) % X
        start = pl.multiple_of(jnp.where(source < x, B_AT, R_AT), 128)
        part = xg.at[source, pl.ds(start, 272)]
        pltpu.make_async_remote_copy(
            src_ref=part, dst_ref=part, send_sem=x_s.at[m], recv_sem=x_r.at[m],
            device_id=at(dx=m), device_id_type=MESH,
        ).wait_recv()
    state, seed = zero, zero
    for j in range(X - 1):
        i = X - 1 - j
        r_j, r_i = xg[j, pl.ds(R_AT, DK), :], xg[i, pl.ds(R_AT, DK), :]
        grown = xg[j, pl.ds(B_AT, DK), :].astype(F32)
        if j:
            grown = grown + scale_of(xg.at[j]) * state + dot(r_j, state)
        state = jnp.where(j < x, grown, state)
        grown = xg[i, pl.ds(Z_AT, DK), :].astype(F32)
        if j:
            grown = grown + scale_of(xg.at[i]) * seed + dot(r_i, seed, 0, 0)
        seed = jnp.where(i > x, grown, seed)
    s_in = a_pre * state + dot(r_pre, state) + b_pre
    g_out = a_suf * seed + dot(t_suf, seed) + z_suf

    w = w0 - dot(xs, s_in)
    yy = y0 + dot(xf, g_out)
    wb, yb = w.astype(BF16), yy.astype(BF16)
    s_hi, s_lo = split(s_in)
    e = jnp.where(causal, decay * dot(g, wb, 1, 1), 0.0)
    et = jnp.where(anti, decay * dot(wb, g, 1, 1), 0.0)
    h = jnp.where(rows > cols, dot(yb, wb, 1, 1), dot(wb, yb, 1, 1)) * decay
    h = jnp.where(rows == cols, 0.0, h)
    dq = opening * (dot(g, s_hi, 1, 1) + dot(g, s_lo, 1, 1)) + dot(e, kb)
    dk = fading * dot(wb, g_out, 1, 1) + dot(et, qb) - dot(h, kb) - opening * dot(yb, s_hi, 1, 1)
    dq = q_inv * (dq - qn * jnp.sum(qn * dq, axis=1, keepdims=True))
    dk = k_inv * (dk - kn * jnp.sum(kn * dk, axis=1, keepdims=True))
    grads = jnp.concatenate([dq, dk, yy], axis=1).astype(BF16)

    def core_copy(turn):
        return pltpu.make_async_remote_copy(
            src_ref=core_out.at[turn], dst_ref=core_in.at[turn], send_sem=c_s.at[turn],
            recv_sem=c_r.at[turn], device_id=at(dc=1), device_id_type=MESH,
        )

    def z_copy(hop):
        turn, start, size, to = HOPS[hop]
        part = pl.ds(start, size)
        return pltpu.make_async_remote_copy(
            src_ref=z_out.at[turn, part], dst_ref=z_in.at[turn, part], send_sem=z_s.at[hop],
            recv_sem=z_r.at[hop], device_id=at(dz=to), device_id_type=MESH,
        )

    def product(turn):
        to = pl.multiple_of(((z + ORDER[turn] + Z) % Z) * 2 * DK, 2 * DK)
        weight = weights(pl.ds(to, 2 * DK))
        both = dot(grads, weight, 1, 1)
        left, right = both[:, :DK], both[:, DK:]
        core_out[turn] = jnp.where(core == 0, right, left).astype(BF16)
        core_copy(turn).start()
        own[turn] = jnp.where(core == 0, left, right)

    def pass_on(turn):
        core_copy(turn).wait_recv()
        z_out[turn] = (own[turn] + core_in[turn].astype(F32)).astype(BF16)
        for hop in SENDS[turn]:
            z_copy(hop).start()

    for turn in range(Z):
        product(turn)
        if LAG <= turn < LAG + 5:
            pass_on(turn - LAG)
    core_copy(5).wait_recv()
    core_copy(6).wait_recv()
    for hop, joins in ADDS:
        turn, start, size, _ = HOPS[hop]
        part = pl.ds(start, size)
        mine = own[turn, part, :] + core_in[turn, part, :].astype(F32)
        for other in joins:
            z_copy(other).wait_recv()
            mine = mine + z_in[HOPS[other][0], part, :].astype(F32)
        z_out[turn, part, :] = mine.astype(BF16)
        z_copy(hop).start()
    core_copy(Z - 1).wait_recv()
    z_copy(6).wait_recv()
    z_copy(7).wait_recv()
    mine = own[Z - 1] + core_in[Z - 1].astype(F32) + z_in[3].astype(F32) + z_in[4].astype(F32)
    for hop in (9, 10, 8, 11):
        z_copy(hop).wait_recv()
    mine = mine + z_in[5].astype(F32) + z_in[6].astype(F32)
    out[...] = mine.astype(BF16)

    for piece in range(3):
        pair_copy(piece, odd).wait_send()
    for piece in range(3):
        for m in (1, 2, 3):
            row_copy(m, piece, behind_us if m == 3 else pair).wait_send()
    for copy in x_copies:
        copy.wait_send()
    for turn in range(Z):
        core_copy(turn).wait_send()
    for hop in range(len(HOPS)):
        z_copy(hop).wait_send()


def on_device(tokens, qkv_weight, beta_logit, log_decay, out_grad):
    dma = pltpu.SemaphoreType.DMA
    return pl.pallas_call(
        kernel,
        out_shape=jax.ShapeDtypeStruct((C, DK), BF16),
        in_specs=[pl.BlockSpec(memory_space=pl.ANY)] * 5,
        out_specs=pl.BlockSpec(memory_space=pltpu.VMEM),
        scratch_shapes=[
            pltpu.VMEM((C, K_PARTS * K_PART), BF16),
            pltpu.VMEM((3, K_PARTS * K_PART, DK), BF16),
            pltpu.VMEM((1, C), F32),
            pltpu.VMEM((1, C), F32),
            pltpu.VMEM((C, DK), BF16),
            pltpu.VMEM((2, ROWS, DK), BF16),
            pltpu.VMEM((4, ROWS, DK), BF16),
            pltpu.VMEM((X, ROWS, DK), BF16),
            pltpu.VMEM((Z, C, DK), BF16),
            pltpu.VMEM((Z, C, DK), BF16),
            pltpu.VMEM((Z, C, DK), F32),
            pltpu.VMEM((Z - 1, C, DK), BF16),
            pltpu.VMEM((Z - 1, C, DK), BF16),
            dma((3 + K_PARTS,)), dma((K_PARTS, 3)),
            dma((3,)), dma((3,)), dma((3, 3)), dma((3, 3)), dma((X,)), dma((X,)),
            dma((Z,)), dma((Z,)), dma((len(HOPS),)), dma((len(HOPS),)),
        ],
        compiler_params=pltpu.CompilerParams(
            collective_id=0, has_side_effects=True, vmem_limit_bytes=63 * 2**20
        ),
        name="delta_rule",
    )(tokens, qkv_weight, beta_logit, log_decay, out_grad)


def solution(mesh):
    return jax.shard_map(
        on_device,
        mesh=mesh,
        in_specs=(
            P("seq", None),
            P(None, None, "head"),
            P("head", "seq"),
            P("head", "seq"),
            P("seq", "head"),
        ),
        out_specs=P("seq", "head"),
        check_vma=False,
    )
```

```python
import functools

import jax
import jax.numpy as jnp
from jax import lax
from jax.experimental import pallas as pl
from jax.experimental.pallas import tpu as pltpu
from jax.sharding import PartitionSpec as P

F32 = jnp.float32
BF16 = jnp.bfloat16
MESH = pl.DeviceIdType.MESH
X, Y, Z = 4, 8, 8
C, DK = 256, 128
B_AT, R_AT, A_AT, Z_AT, ROWS = 0, 128, 256, 272, 400
PIECES = ((R_AT, 144), (B_AT, 128), (Z_AT, 128))
K_PARTS, K_PART = 2, 1024
ORDER = (4, 3, -3, 1, -1, 2, -2, 0)
HOPS = (
    (0, 0, 128, 2), (0, 128, 128, -2),
    (1, 0, 128, 1), (1, 128, 128, 1), (2, 0, 128, -1), (2, 128, 128, -1),
    (3, 0, 256, 1), (4, 0, 256, -1),
    (5, 0, 128, 2), (5, 128, 128, 2), (6, 0, 128, -2), (6, 128, 128, -2),
)
SENDS = ((0, 1), (3, 2), (4, 5), (6,), (7,))
ADDS = ((9, (3,)), (10, (4,)), (8, (0, 2)), (11, (1, 5)))
LAG = 3


def dot(a, b, ca=1, cb=0):
    return lax.dot_general(
        a.astype(BF16), b.astype(BF16), (((ca,), (cb,)), ((), ())), preferred_element_type=F32
    )


def split(a):
    upper = a.astype(BF16)
    return upper, (a - upper.astype(F32)).astype(BF16)


def thirds(a):
    upper, rest = split(a)
    middle = rest
    lower = (a - upper.astype(F32) - middle.astype(F32)).astype(BF16)
    return upper, middle, lower


def unit_inverse_less_identity(low, rows, cols):
    def same(shift):
        return (rows >> shift) == (cols >> shift)

    power = jnp.where(same(5), low, 0.0)
    off = -power
    for _ in range(4):
        power = dot(power, power)
        off = off + power + dot(off, power)
    for shift in (5, 6, 7):
        inside = jnp.where(same(shift + 1) & ~same(shift), low, 0.0)
        left = inside + dot(off, inside)
        off = off - left - dot(left, off)
    return off


def kernel(
    tok_hbm, wgt_hbm, bl_hbm, ld_hbm, og_hbm, out,
    tok, wgt, bl, ld, og, ag, qg, xg, core_out, core_in, own, z_out, z_in,
    in_sem, w_sem, a_s, a_r, q_s, q_r, x_s, x_r, c_s, c_r, z_s, z_r,
):
    seq, head = lax.axis_index("seq"), lax.axis_index("head")
    x, y = seq // Y, seq % Y
    z, core = head // 2, head % 2

    def at(dx=0, dy=0, dz=0, dc=0):
        return (
            ((x + dx) % X) * Y + (y + dy + Y) % Y,
            ((z + dz + Z) % Z) * 2 + (core + dc) % 2,
        )

    small = [
        pltpu.make_async_copy(src, dst, in_sem.at[i])
        for i, (src, dst) in enumerate(((ld_hbm, ld), (bl_hbm, bl), (og_hbm, og)))
    ]
    parts = []
    for k in range(K_PARTS):
        rows_k = pl.ds(k * K_PART, K_PART)
        parts.append(
            [pltpu.make_async_copy(tok_hbm.at[:, rows_k], tok.at[:, rows_k], in_sem.at[3 + k])]
            + [
                pltpu.make_async_copy(
                    wgt_hbm.at[p, rows_k, :], wgt.at[p, rows_k, :], w_sem.at[k, p]
                )
                for p in range(3)
            ]
        )
    for copy in small[:2] + sum(parts, []) + small[2:]:
        copy.start()
    pair, odd = y // 2, y % 2
    way = 2 * odd - 1
    peers = [at(dy=m * way) for m in (-2, -1, 1, 2)]
    peers += [at(dx=m) for m in (1, 2, 3)] + [at(dc=1)] + [at(dz=m) for m in (-2, -1, 1, 2)]
    barrier = pltpu.get_barrier_semaphore()
    for peer in peers:
        pl.semaphore_signal(barrier, inc=1, device_id=peer, device_id_type=MESH)

    rows = lax.broadcasted_iota(jnp.int32, (C, C), 0)
    cols = lax.broadcasted_iota(jnp.int32, (C, C), 1)
    causal, anti = rows >= cols, rows <= cols
    small[0].wait()
    small[1].wait()
    beta_row = 1.0 / (1.0 + jnp.exp(-bl[...]))
    beta = jnp.sum(jnp.where(rows == cols, beta_row, 0.0), axis=1, keepdims=True)
    cum = jnp.sum(jnp.where(cols <= rows, ld[...], 0.0), axis=1, keepdims=True)
    cum_row = jnp.sum(jnp.where(rows == cols, cum, 0.0), axis=0, keepdims=True)
    total = cum[C - 1 : C, :]
    decay = jnp.exp(-jnp.abs(cum - cum_row))
    opening = jnp.exp(cum)
    fading = jnp.exp(total - cum)

    def weights(at_rows):
        return jnp.concatenate([wgt[p, at_rows, :] for p in range(3)], axis=1)

    proj = None
    for k in range(K_PARTS):
        for copy in parts[k]:
            copy.wait()
        rows_k = pl.ds(k * K_PART, K_PART)
        term = jnp.dot(tok[:, rows_k], weights(rows_k), preferred_element_type=F32)
        proj = term if proj is None else proj + term
    small[2].wait()
    q, key, v = proj[:, :DK], proj[:, DK : 2 * DK], proj[:, 2 * DK :]
    q_inv = lax.rsqrt(jnp.sum(q * q, axis=1, keepdims=True) + 1e-6)
    k_inv = lax.rsqrt(jnp.sum(key * key, axis=1, keepdims=True) + 1e-6)
    qn, kn = q * q_inv, key * k_inv
    g = og[...]

    kb = kn.astype(BF16)
    qb = qn.astype(BF16)
    low = beta * jnp.where(rows > cols, decay * dot(kb, kb, 1, 1), 0.0)
    off = unit_inverse_less_identity(low, rows, cols).astype(BF16)
    bk = opening * kn
    fk = fading * kn
    x0 = beta * bk
    xs = x0 + dot(off, x0)
    xf = beta * (fk + dot(off, fk, 0, 0))
    r_seg = -dot(xf, bk, 0, 0)
    a_seg = jnp.broadcast_to(jnp.exp(total), (1, DK))

    def put_r(ref, a, r):
        ref[pl.ds(R_AT, DK), :] = r.astype(BF16)
        place = lax.broadcasted_iota(jnp.int32, (16, DK), 0)
        first, second, third = [t.astype(F32) for t in thirds(a)]
        tile = jnp.where(place == 0, first, jnp.where(place == 1, second, jnp.where(place == 2, third, 0.0)))
        ref[pl.ds(A_AT, 16), :] = tile.astype(BF16)

    def put(ref, a, r, b, zz):
        put_r(ref, a, r)
        ref[pl.ds(B_AT, DK), :] = b.astype(BF16)
        ref[pl.ds(Z_AT, DK), :] = zz.astype(BF16)

    def scale_of(ref):
        return jnp.sum(ref[pl.ds(A_AT, 16), :].astype(F32), axis=0, keepdims=True)

    def pair_copy(piece, slot):
        start, size = PIECES[piece]
        part = ag.at[slot, pl.ds(start, size)]
        return pltpu.make_async_remote_copy(
            src_ref=part, dst_ref=part, send_sem=a_s.at[piece], recv_sem=a_r.at[piece],
            device_id=at(dy=-way), device_id_type=MESH,
        )

    put_r(ag.at[odd], a_seg, r_seg)
    pl.semaphore_wait(barrier, len(peers))
    pair_copy(0, odd).start()
    v0 = beta * v
    w0 = v0 + dot(off, v0)
    fk_hi, fk_lo = split(fk)
    w_hi, w_lo = split(w0)
    b_seg = dot(fk_hi, w_hi, 0, 0) + (dot(fk_lo, w_hi, 0, 0) + dot(fk_hi, w_lo, 0, 0))
    ag[odd, pl.ds(B_AT, DK), :] = b_seg.astype(BF16)
    pair_copy(1, odd).start()
    pg = dot(jnp.where(anti, decay * dot(kb, qb, 1, 1), 0.0), g)
    z_seg = dot(opening * qn, g, 0, 0) - dot(xs, pg, 0, 0)
    ag[odd, pl.ds(Z_AT, DK), :] = z_seg.astype(BF16)
    pair_copy(2, odd).start()
    y0 = beta * (pg + dot(off, pg, 0, 0))

    def leaf(ref):
        r = ref[pl.ds(R_AT, DK), :].astype(F32)
        return (
            scale_of(ref), r, r.T, ref[pl.ds(B_AT, DK), :].astype(F32), ref[pl.ds(Z_AT, DK), :].astype(F32)
        )

    def wide(left, right):
        return jnp.concatenate([left, right], axis=1)

    def ahead(early, late):
        a0, r0, _, b0, _ = early
        a1, r1, _, b1, _ = late
        both = dot(r1, wide(r0, b0))
        return a0 * a1, a1 * r0 + a0 * r1 + both[:, :DK], a1 * b0 + b1 + both[:, DK:]

    def behind(early, late):
        a0, _, t0, _, z0 = early
        a1, _, t1, _, z1 = late
        both = dot(t0, wide(t1, z1))
        return a0 * a1, a1 * t0 + a0 * t1 + both[:, :DK], a0 * z1 + z0 + both[:, DK:]

    def compose(early, late):
        a, r, b = ahead(early, late)
        _, t, zz = behind(early, late)
        return a, r, t, b, zz

    def pick(flag, one, other):
        return tuple(jnp.where(flag, p, o) for p, o in zip(one, other))

    def row_copy(m, piece, slot):
        start, size = PIECES[piece]
        part = qg.at[slot, pl.ds(start, size)]
        return pltpu.make_async_remote_copy(
            src_ref=part, dst_ref=part, send_sem=q_s.at[m - 1, piece], recv_sem=q_r.at[m - 1, piece],
            device_id=at(dy=(2 if m == 2 else 1) * way), device_id_type=MESH,
        )

    def send_pair(piece):
        for m in (2, 1):
            row_copy(m, piece, pair).start()

    pair_copy(0, 1 - odd).wait_recv()
    a_0, a_1 = scale_of(ag.at[0]), scale_of(ag.at[1])
    r_0, r_1 = ag[0, pl.ds(R_AT, DK), :], ag[1, pl.ds(R_AT, DK), :]
    r_pair = a_1 * r_0.astype(F32) + a_0 * r_1.astype(F32) + dot(r_1, r_0)
    put_r(qg.at[pair], a_0 * a_1, r_pair)
    send_pair(0)
    pair_copy(1, 1 - odd).wait_recv()
    b_0 = ag[0, pl.ds(B_AT, DK), :]
    b_pair = a_1 * b_0.astype(F32) + ag[1, pl.ds(B_AT, DK), :].astype(F32) + dot(r_1, b_0)
    qg[pair, pl.ds(B_AT, DK), :] = b_pair.astype(BF16)
    send_pair(1)
    pair_copy(2, 1 - odd).wait_recv()
    z_1 = ag[1, pl.ds(Z_AT, DK), :]
    z_pair = a_0 * z_1.astype(F32) + ag[0, pl.ds(Z_AT, DK), :].astype(F32) + dot(r_0, z_1, 0, 0)
    qg[pair, pl.ds(Z_AT, DK), :] = z_pair.astype(BF16)
    send_pair(2)
    early, late = leaf(ag.at[0]), leaf(ag.at[1])
    behind_us = (pair - way + 4) % 4
    for piece in range(3):
        row_copy(2, piece, behind_us).wait_recv()
        row_copy(3, piece, behind_us).start()
    for piece in range(3):
        row_copy(1, piece, (pair + way + 4) % 4).wait_recv()
    for piece in range(3):
        row_copy(3, piece, (pair + 2) % 4).wait_recv()
    pairs = [leaf(qg.at[j]) for j in range(4)]
    quads = [compose(pairs[0], pairs[1]), compose(pairs[2], pairs[3])]
    a_row, r_row, b_row = ahead(quads[0], quads[1])
    _, _, z_row = behind(quads[0], quads[1])

    put(xg.at[x], a_row, r_row, b_row, z_row)
    x_copies = []
    for m in (2, 1, 3):
        start = pl.multiple_of(jnp.where(x + m < X, B_AT, R_AT), 128)
        part = xg.at[x, pl.ds(start, 272)]
        x_copies.append(
            pltpu.make_async_remote_copy(
                src_ref=part, dst_ref=part, send_sem=x_s.at[m], recv_sem=x_r.at[m],
                device_id=at(dx=m), device_id_type=MESH,
            )
        )
        x_copies[-1].start()

    zero = jnp.zeros((DK, DK), F32)
    none = (jnp.ones((1, DK), F32), zero, zero, zero, zero)
    four, two, one = y >= 4, y % 4 >= 2, y % 2 == 1
    before = pick(four, quads[0], none)
    second = pick(two, pick(four, pairs[2], pairs[0]), none)
    third = pick(one, early, none)
    a_pre, r_pre, b_pre = ahead(before, second)
    a_pre, r_pre, b_pre = ahead((a_pre, r_pre, None, b_pre, None), third)
    first = pick(one, none, late)
    second = pick(two, none, pick(four, pairs[3], pairs[1]))
    last = pick(four, none, quads[1])
    a_suf, t_suf, z_suf = behind(second, last)
    a_suf, t_suf, z_suf = behind(first, (a_suf, None, t_suf, None, z_suf))

    for m in (1, 3, 2):
        source = (x - m + X) % X
        start = pl.multiple_of(jnp.where(source < x, B_AT, R_AT), 128)
        part = xg.at[source, pl.ds(start, 272)]
        pltpu.make_async_remote_copy(
            src_ref=part, dst_ref=part, send_sem=x_s.at[m], recv_sem=x_r.at[m],
            device_id=at(dx=m), device_id_type=MESH,
        ).wait_recv()
    state, seed = zero, zero
    for j in range(X - 1):
        i = X - 1 - j
        r_j, r_i = xg[j, pl.ds(R_AT, DK), :], xg[i, pl.ds(R_AT, DK), :]
        grown = xg[j, pl.ds(B_AT, DK), :].astype(F32)
        if j:
            grown = grown + scale_of(xg.at[j]) * state + dot(r_j, state)
        state = jnp.where(j < x, grown, state)
        grown = xg[i, pl.ds(Z_AT, DK), :].astype(F32)
        if j:
            grown = grown + scale_of(xg.at[i]) * seed + dot(r_i, seed, 0, 0)
        seed = jnp.where(i > x, grown, seed)
    s_in = a_pre * state + dot(r_pre, state) + b_pre
    g_out = a_suf * seed + dot(t_suf, seed) + z_suf

    w = w0 - dot(xs, s_in)
    yy = y0 + dot(xf, g_out)
    wb, yb = w.astype(BF16), yy.astype(BF16)
    s_hi, s_lo = split(s_in)
    e = jnp.where(causal, decay * dot(g, wb, 1, 1), 0.0)
    et = jnp.where(anti, decay * dot(wb, g, 1, 1), 0.0)
    h = jnp.where(rows > cols, dot(yb, wb, 1, 1), dot(wb, yb, 1, 1)) * decay
    h = jnp.where(rows == cols, 0.0, h)
    dq = opening * (dot(g, s_hi, 1, 1) + dot(g, s_lo, 1, 1)) + dot(e, kb)
    dk = fading * dot(wb, g_out, 1, 1) + dot(et, qb) - dot(h, kb) - opening * dot(yb, s_hi, 1, 1)
    dq = q_inv * (dq - qn * jnp.sum(qn * dq, axis=1, keepdims=True))
    dk = k_inv * (dk - kn * jnp.sum(kn * dk, axis=1, keepdims=True))
    grads = jnp.concatenate([dq, dk, yy], axis=1).astype(BF16)

    def core_copy(turn):
        return pltpu.make_async_remote_copy(
            src_ref=core_out.at[turn], dst_ref=core_in.at[turn], send_sem=c_s.at[turn],
            recv_sem=c_r.at[turn], device_id=at(dc=1), device_id_type=MESH,
        )

    def z_copy(hop):
        turn, start, size, to = HOPS[hop]
        part = pl.ds(start, size)
        return pltpu.make_async_remote_copy(
            src_ref=z_out.at[turn, part], dst_ref=z_in.at[turn, part], send_sem=z_s.at[hop],
            recv_sem=z_r.at[hop], device_id=at(dz=to), device_id_type=MESH,
        )

    def product(turn):
        to = pl.multiple_of(((z + ORDER[turn] + Z) % Z) * 2 * DK, 2 * DK)
        weight = weights(pl.ds(to, 2 * DK))
        both = dot(grads, weight, 1, 1)
        left, right = both[:, :DK], both[:, DK:]
        core_out[turn] = jnp.where(core == 0, right, left).astype(BF16)
        core_copy(turn).start()
        own[turn] = jnp.where(core == 0, left, right)

    def pass_on(turn):
        core_copy(turn).wait_recv()
        z_out[turn] = (own[turn] + core_in[turn].astype(F32)).astype(BF16)
        for hop in SENDS[turn]:
            z_copy(hop).start()

    for turn in range(Z):
        product(turn)
        if LAG <= turn < LAG + 5:
            pass_on(turn - LAG)
    core_copy(5).wait_recv()
    core_copy(6).wait_recv()
    for hop, joins in ADDS:
        turn, start, size, _ = HOPS[hop]
        part = pl.ds(start, size)
        mine = own[turn, part, :] + core_in[turn, part, :].astype(F32)
        for other in joins:
            z_copy(other).wait_recv()
            mine = mine + z_in[HOPS[other][0], part, :].astype(F32)
        z_out[turn, part, :] = mine.astype(BF16)
        z_copy(hop).start()
    core_copy(Z - 1).wait_recv()
    z_copy(6).wait_recv()
    z_copy(7).wait_recv()
    mine = own[Z - 1] + core_in[Z - 1].astype(F32) + z_in[3].astype(F32) + z_in[4].astype(F32)
    for hop in (9, 10, 8, 11):
        z_copy(hop).wait_recv()
    mine = mine + z_in[5].astype(F32) + z_in[6].astype(F32)
    out[...] = mine.astype(BF16)

    for piece in range(3):
        pair_copy(piece, odd).wait_send()
    for piece in range(3):
        for m in (1, 2, 3):
            row_copy(m, piece, behind_us if m == 3 else pair).wait_send()
    for copy in x_copies:
        copy.wait_send()
    for turn in range(Z):
        core_copy(turn).wait_send()
    for hop in range(len(HOPS)):
        z_copy(hop).wait_send()


def on_device(tokens, qkv_weight, beta_logit, log_decay, out_grad):
    dma = pltpu.SemaphoreType.DMA
    return pl.pallas_call(
        kernel,
        out_shape=jax.ShapeDtypeStruct((C, DK), BF16),
        in_specs=[pl.BlockSpec(memory_space=pl.ANY)] * 5,
        out_specs=pl.BlockSpec(memory_space=pltpu.VMEM),
        scratch_shapes=[
            pltpu.VMEM((C, K_PARTS * K_PART), BF16),
            pltpu.VMEM((3, K_PARTS * K_PART, DK), BF16),
            pltpu.VMEM((1, C), F32),
            pltpu.VMEM((1, C), F32),
            pltpu.VMEM((C, DK), BF16),
            pltpu.VMEM((2, ROWS, DK), BF16),
            pltpu.VMEM((4, ROWS, DK), BF16),
            pltpu.VMEM((X, ROWS, DK), BF16),
            pltpu.VMEM((Z, C, DK), BF16),
            pltpu.VMEM((Z, C, DK), BF16),
            pltpu.VMEM((Z, C, DK), F32),
            pltpu.VMEM((Z - 1, C, DK), BF16),
            pltpu.VMEM((Z - 1, C, DK), BF16),
            dma((3 + K_PARTS,)), dma((K_PARTS, 3)),
            dma((3,)), dma((3,)), dma((3, 3)), dma((3, 3)), dma((X,)), dma((X,)),
            dma((Z,)), dma((Z,)), dma((len(HOPS),)), dma((len(HOPS),)),
        ],
        compiler_params=pltpu.CompilerParams(
            collective_id=0, has_side_effects=True, vmem_limit_bytes=63 * 2**20
        ),
        name="delta_rule",
    )(tokens, qkv_weight, beta_logit, log_decay, out_grad)


def solution(mesh):
    return jax.shard_map(
        on_device,
        mesh=mesh,
        in_specs=(
            P("seq", None),
            P(None, None, "head"),
            P("head", "seq"),
            P("head", "seq"),
            P("seq", "head"),
        ),
        out_specs=P("seq", "head"),
        check_vma=False,
    )
```
